128 devices in a mesh: col: 16 (over y, z), row: 8 (over x, core).
Axes of the slice: x: 4, y: 4, z: 4, core: 2. Of those that a mesh axis runs over, the one named last changes fastest.
Arguments:
- tiles: bfloat16 [2, 8192, 16384], P(None, 'row', 'col')
- extents: int32 [2, 8, 16], replicated, may hold values from 32 to 128
- offsets: int32 [2, 8, 16], replicated, may hold values from 0 to 127, as said below
- bands: int32 [2, 8, 16], replicated, may hold values from 0 to 8, as said below
Outputs:
- blended: float32 [2, 8192, 16384], P(None, 'row', 'col')
- weight_total: float32 [8192, 16384], P('row', 'col')
The draws below stay inside these ranges and needn't reach their ends.
Inputs may be any that keep to these rules, and one draw needn't show every extreme that they name: Some tile has both offsets equal to 127 and some tile has both equal to 0. `bands`: entry 0 of a tile is smaller than entry 1; some tile has the band 0 to 8.
All inputs are finite; a program needn't handle non-finite values.
Results may differ from the reference program's by a relative error of at most 0.0003.
Values may be sent and summed in bfloat16 or wider, within the bound.
A program may use at most 128 MiB of HBM per device.

```python
import jax
import jax.numpy as jnp
from jax import lax

PLANES = 2
TILE = 1024
STRIP = 128
SPILL = 128
BLOCK = 128
GRID_ROWS = 8
GRID_COLS = 16
ROWS_PX = 8192
COLS_PX = 16384
N_COL = 16
N_ROW = 8


def draw_tiles(key, part):
    grid_rows = ROWS_PX // TILE
    grid_cols = COLS_PX // TILE
    subkeys = jax.random.split(key, 9)
    full_shape = (PLANES, grid_rows, TILE, grid_cols, TILE)
    base_noise = jax.random.normal(subkeys[0], full_shape, jnp.float32)
    spread = 0.7
    horiz_share = jax.random.normal(subkeys[1], (PLANES, grid_rows, TILE, grid_cols, STRIP), jnp.float32)
    horiz_share = horiz_share * jax.random.uniform(subkeys[2], (PLANES, grid_rows, 1, grid_cols, 1), jnp.float32, 0.5, 2.0)
    vert_share = jax.random.normal(subkeys[3], (PLANES, grid_rows, STRIP, grid_cols, TILE), jnp.float32)
    vert_share = vert_share * jax.random.uniform(subkeys[4], (PLANES, grid_rows, 1, grid_cols, 1), jnp.float32, 0.5, 2.0)
    horiz_left = jnp.concatenate([jnp.zeros((PLANES, grid_rows, TILE, 1, STRIP), jnp.float32), horiz_share[:, :, :, :-1, :]], axis=3)
    horiz_field = jnp.concatenate([horiz_left, jnp.zeros((PLANES, grid_rows, TILE, grid_cols, TILE - 2 * STRIP), jnp.float32), horiz_share], axis=4)
    vert_top = jnp.concatenate([jnp.zeros((PLANES, 1, STRIP, grid_cols, TILE), jnp.float32), vert_share[:, :-1]], axis=1)
    vert_field = jnp.concatenate([vert_top, jnp.zeros((PLANES, grid_rows, TILE - 2 * STRIP, grid_cols, TILE), jnp.float32), vert_share], axis=2)
    row_factor = jnp.exp(jax.random.uniform(subkeys[5], (PLANES, grid_rows, TILE, grid_cols, 1), jnp.float32, -0.4, 0.4))
    col_factor = jnp.exp(jax.random.uniform(subkeys[6], (PLANES, grid_rows, 1, grid_cols, TILE), jnp.float32, -0.4, 0.4))
    tile_gain = jnp.exp(jax.random.uniform(subkeys[7], (PLANES, grid_rows, 1, grid_cols, 1), jnp.float32, -spread, spread))
    tile_offset = jax.random.uniform(subkeys[8], (PLANES, grid_rows, 1, grid_cols, 1), jnp.float32, -1.0, 1.0)
    values = tile_gain * row_factor * col_factor * (base_noise + horiz_field + vert_field) + tile_offset
    return values.reshape(PLANES, ROWS_PX, COLS_PX).astype(jnp.bfloat16)


def draw_offsets(key, part):
    grid_rows = ROWS_PX // TILE
    grid_cols = COLS_PX // TILE
    count_tiles = grid_rows * grid_cols
    values = jax.random.randint(key, (2, count_tiles), 0, SPILL, dtype=jnp.int32)
    chosen = jax.random.randint(jax.random.fold_in(key, 7), (), 0, count_tiles, dtype=jnp.int32)
    tile_ids = jnp.arange(count_tiles, dtype=jnp.int32)
    values = jnp.where(tile_ids[None, :] == chosen, SPILL - 1, values)
    values = jnp.where(tile_ids[None, :] == (chosen + 1) % count_tiles, 0, values)
    return values.reshape(2, grid_rows, grid_cols)


def draw_bands(key, part):
    grid_rows = ROWS_PX // TILE
    grid_cols = COLS_PX // TILE
    count_tiles = grid_rows * grid_cols
    blocks = TILE // BLOCK
    band_low = jax.random.randint(jax.random.fold_in(key, 1), (count_tiles,), 0, (blocks + 1) // 2, dtype=jnp.int32)
    band_high = blocks - jax.random.randint(jax.random.fold_in(key, 2), (count_tiles,), 0, blocks // 2, dtype=jnp.int32)
    chosen = jax.random.randint(jax.random.fold_in(key, 3), (), 0, count_tiles, dtype=jnp.int32)
    tile_ids = jnp.arange(count_tiles, dtype=jnp.int32)
    band_low = jnp.where(tile_ids == chosen, 0, band_low)
    band_high = jnp.where(tile_ids == chosen, blocks, band_high)
    return jnp.stack([band_low, band_high]).reshape(2, grid_rows, grid_cols)


def set_ends(entries, own_key, smallest, high):
    longest = entries.shape.index(max(entries.shape))
    spots = []
    for shift in (0, 1):
        where = [jax.random.randint(jax.random.fold_in(own_key, axis), (), 0, length) for axis, length in enumerate(entries.shape)]
        where[longest] = (where[longest] + shift) % entries.shape[longest]
        spots.append(tuple(where))
    return entries.at[spots[0]].set(smallest).at[spots[1]].set(high)


def setup_inputs(seed: int = 0) -> dict:
    key_list = jax.random.split(jax.random.key(seed), 5)
    return {
        "tiles": draw_tiles(jax.random.fold_in(key_list[4], 71), 0),
        "extents": set_ends(jax.random.randint(key_list[1], (2, GRID_ROWS, GRID_COLS), STRIP // 4, STRIP + 1), jax.random.fold_in(key_list[1], 1), STRIP // 4, STRIP).astype(jnp.int32),
        "offsets": draw_offsets(jax.random.fold_in(key_list[4], 71), 0),
        "bands": draw_bands(jax.random.fold_in(key_list[4], 71), 0),
    }


eps = 1e-6


def pair_terms(former, latter, window):
    full_window = jnp.broadcast_to(window, former.shape)
    number = jnp.sum(full_window, axis=(-2, -1), keepdims=True)
    mean_former = jnp.sum(former * full_window, axis=(-2, -1), keepdims=True) / number
    mean_latter = jnp.sum(latter * full_window, axis=(-2, -1), keepdims=True) / number
    dev_former = (former - mean_former) * full_window
    dev_latter = (latter - mean_latter) * full_window
    flat_number = number[..., 0, 0]
    var_former = jnp.sum(dev_former * dev_former, axis=(-2, -1)) / flat_number
    var_latter = jnp.sum(dev_latter * dev_latter, axis=(-2, -1)) / flat_number
    covariance = jnp.sum(dev_former * dev_latter, axis=(-2, -1)) / flat_number
    weight = covariance * covariance / ((var_former + eps) * (var_latter + eps))
    log_ratio = 0.25 * (jnp.log(var_latter + eps) - jnp.log(var_former + eps))
    shift_term = 0.5 * (mean_latter - mean_former)[..., 0, 0]
    return weight, weight * log_ratio, weight * shift_term


def combine(right_pair, down_pair, left_pair, upper_pair):
    denominator = 1.0 + right_pair[0] + down_pair[0] + left_pair[0] + upper_pair[0]
    log_gain = (right_pair[1] + down_pair[1] - left_pair[1] - upper_pair[1]) / denominator
    offset = (right_pair[2] + down_pair[2] - left_pair[2] - upper_pair[2]) / denominator
    return log_gain, offset


def blend_weight(row_ids, col_ids, band_low, band_high, tile_px):
    half = tile_px / 2.0
    row_fade = (jnp.minimum(row_ids, tile_px - 1 - row_ids) + 1).astype(jnp.float32) / half
    col_fade = (jnp.minimum(col_ids, tile_px - 1 - col_ids) + 1).astype(jnp.float32) / half
    live = ((row_ids >= band_low * BLOCK) & (row_ids < band_high * BLOCK)).astype(jnp.float32)
    return (live * row_fade)[:, None] * col_fade[None, :]


def make_contrib(raw_data, log_gain, offset, row_ids, col_ids, band_low, band_high, tile_px):
    weight = blend_weight(row_ids, col_ids, band_low, band_high, tile_px)
    values = (jnp.exp(log_gain)[:, None, None] * raw_data.astype(jnp.float32) + offset[:, None, None]) * weight[None]
    return jnp.concatenate([values, weight[None]], axis=0)


def add_at(canvas, contrib, top_row, left_col):
    start = (jnp.zeros((), jnp.int32), top_row.astype(jnp.int32), left_col.astype(jnp.int32))
    current = lax.dynamic_slice(canvas, start, contrib.shape)
    return lax.dynamic_update_slice(canvas, current + contrib, start)


def tile_terms(horiz_terms, vert_terms):
    first_h = tuple(jnp.pad(item, ((0, 0), (0, 1), (0, 0))) for item in horiz_terms)
    second_h = tuple(jnp.pad(item, ((0, 0), (1, 0), (0, 0))) for item in horiz_terms)
    first_v = tuple(jnp.pad(item, ((0, 1), (0, 0), (0, 0))) for item in vert_terms)
    second_v = tuple(jnp.pad(item, ((1, 0), (0, 0), (0, 0))) for item in vert_terms)
    return combine(first_h, first_v, second_h, second_v)


def reference(tiles, extents, offsets, bands):
    tile_grid = tiles.reshape(PLANES, N_ROW, TILE, N_COL, TILE).transpose(1, 3, 0, 2, 4)
    strip_ids = jnp.arange(STRIP, dtype=jnp.int32)
    horiz_window = (strip_ids[None, None, :] < extents[0, :, :-1, None]).astype(jnp.float32)[:, :, None, None, :]
    vert_window = (strip_ids[None, None, :] < extents[1, :-1, :, None]).astype(jnp.float32)[:, :, None, :, None]
    horiz_first = tile_grid[:, :-1, :, :, TILE - STRIP:].astype(jnp.float32)
    horiz_second = tile_grid[:, 1:, :, :, :STRIP].astype(jnp.float32)
    vert_first = tile_grid[:-1, :, :, TILE - STRIP:, :].astype(jnp.float32)
    vert_second = tile_grid[1:, :, :, :STRIP, :].astype(jnp.float32)
    gain_one, level_one = tile_terms(pair_terms(horiz_first, horiz_second, horiz_window),
                                     pair_terms(vert_first, vert_second, vert_window))

    def corrected(strips, gain_part, level_part):
        return jnp.exp(gain_part)[..., None, None] * strips + level_part[..., None, None]

    horiz_terms = pair_terms(corrected(horiz_first, gain_one[:, :-1], level_one[:, :-1]),
                             corrected(horiz_second, gain_one[:, 1:], level_one[:, 1:]), horiz_window)
    vert_terms = pair_terms(corrected(vert_first, gain_one[:-1], level_one[:-1]),
                            corrected(vert_second, gain_one[1:], level_one[1:]), vert_window)
    gain_two, level_two = tile_terms(horiz_terms, vert_terms)
    log_gain = gain_one + gain_two
    level = jnp.exp(gain_two) * level_one + level_two
    everything = jnp.arange(TILE, dtype=jnp.int32)
    canvas = jnp.zeros((PLANES + 1, ROWS_PX + SPILL, COLS_PX + SPILL), jnp.float32)

    def place_tile(tile_index, canvas):
        grid_row = tile_index // N_COL
        grid_col = tile_index % N_COL
        raw_data = lax.dynamic_index_in_dim(lax.dynamic_index_in_dim(tile_grid, grid_row, 0, False), grid_col, 0, False)
        contrib = make_contrib(raw_data, log_gain[grid_row, grid_col], level[grid_row, grid_col], everything, everything,
                               bands[0, grid_row, grid_col], bands[1, grid_row, grid_col], TILE)
        return add_at(canvas, contrib, grid_row * TILE + offsets[0, grid_row, grid_col],
                      grid_col * TILE + offsets[1, grid_row, grid_col])

    canvas = lax.fori_loop(jnp.int32(0), jnp.int32(N_ROW * N_COL), place_tile, canvas)
    return canvas[:PLANES, :ROWS_PX, :COLS_PX], canvas[PLANES, :ROWS_PX, :COLS_PX]
```

```python
import jax
import jax.numpy as jnp
from jax import lax
from jax.experimental import pallas as pl
from jax.experimental.pallas import tpu as pltpu
from jax.sharding import PartitionSpec as P

STRIP = 128
SPILL = 128
BLOCK = 128
LANES = 128
PLANES = 2
EPS = 1e-6
MESH = pl.DeviceIdType.MESH
F32 = jnp.float32

RIGHT_1, LEFT_1, DOWN_1, UP_1, RIGHT_2, DOWN_2, CORNER = range(7)
STATS, COV, FIRST, FINAL = 7, 11, 15, 19
COPIES = 22


def rows_of(per_plane):
    return jnp.concatenate(
        [jnp.broadcast_to(jnp.sum(a, keepdims=True), (1, LANES)) for a in per_plane], axis=0
    )


def fold(x):
    return jnp.sum(x.reshape(x.shape[0] // 8, 8, x.shape[1]), axis=0)


def sum_tall(ref, plane, mask, term):
    size = 128

    def body(i, acc):
        x = ref[plane, pl.ds(pl.multiple_of(i * size, size), size), :].astype(F32)
        return acc + fold(term(x))

    acc = lax.fori_loop(0, ref.shape[1] // size, body, jnp.zeros((8, LANES), F32))
    return jnp.where(mask, acc, 0.0)


def sum_wide(ref, plane, extent, term):
    size = 16
    ids = lax.broadcasted_iota(jnp.int32, (size, LANES), 0)

    def body(i, acc):
        x = ref[plane, pl.ds(pl.multiple_of(i * size, size), size), :].astype(F32)
        t = term(x)
        part = sum(t[:, k : k + LANES] for k in range(0, x.shape[1], LANES))
        return acc + fold(jnp.where(ids + i * size < extent, part, 0.0))

    return lax.fori_loop(0, STRIP // size, body, jnp.zeros((8, LANES), F32))


def cov_tall(own, own_start, other, own_mean, other_mean, plane, mask):
    size = 128

    def body(i, acc):
        start = pl.multiple_of(i * size, size)
        x = own[plane, pl.ds(own_start + start, size), :].astype(F32) - own_mean
        y = other[plane, pl.ds(start, size), :].astype(F32) - other_mean
        return acc + fold(x * y)

    acc = lax.fori_loop(0, other.shape[1] // size, body, jnp.zeros((8, LANES), F32))
    return jnp.where(mask, acc, 0.0)


def cov_wide(own, own_start, other, own_mean, other_mean, plane, extent):
    size = 16
    width = other.shape[2]
    ids = lax.broadcasted_iota(jnp.int32, (size, LANES), 0)

    def body(i, acc):
        start = pl.multiple_of(i * size, size)
        x = own[plane, pl.ds(start, size), own_start : own_start + width].astype(F32)
        y = other[plane, pl.ds(start, size), :].astype(F32)
        part = sum(
            (x[:, k : k + LANES] - own_mean) * (y[:, k : k + LANES] - other_mean)
            for k in range(0, width, LANES)
        )
        return acc + fold(jnp.where(ids + i * size < extent, part, 0.0))

    return lax.fori_loop(0, STRIP // size, body, jnp.zeros((8, LANES), F32))


def pair_terms(mean_a, var_a, mean_b, var_b, cov, valid):
    weight = cov * cov / ((var_a + EPS) * (var_b + EPS))
    ratio = 0.25 * (jnp.log(var_b + EPS) - jnp.log(var_a + EPS))
    shift = 0.5 * (mean_b - mean_a)
    return tuple(jnp.where(valid, t, 0.0) for t in (weight, weight * ratio, weight * shift))


def combine(right, left, down, upper):
    total = 1.0 + right[0] + down[0] + left[0] + upper[0]
    log_gain = (right[1] + down[1] - left[1] - upper[1]) / total
    level = (right[2] + down[2] - left[2] - upper[2]) / total
    return log_gain, level


def exchange_kernel(
    extents, tiles, left_in, up_in, corner_in, terms,
    strip_r, strip_l, strip_d, strip_u, half_l, half_r, half_u, half_d,
    stats_out, stats_in, cov_out, cov_in, first_out, first_in, final_out, final_in,
    load_sem, send_sem, recv_sem,
):
    n_col, n_row = lax.axis_size("col"), lax.axis_size("row")
    col, row = lax.axis_index("col"), lax.axis_index("row")
    right, left = lax.rem(col + 1, n_col), lax.rem(col + n_col - 1, n_col)
    down, up = lax.rem(row + 1, n_row), lax.rem(row + n_row - 1, n_row)
    tile = tiles.shape[1]
    half = tile // 2
    edge = tile - STRIP
    four = ({"col": right}, {"col": left}, {"row": down}, {"row": up})
    diag = {"col": right, "row": down}
    back = {"col": left, "row": up}

    barrier = pltpu.get_barrier_semaphore()
    for place in (*four, diag, back):
        pl.semaphore_signal(barrier, inc=1, device_id=place, device_id_type=MESH)

    own = (strip_r, strip_l, strip_d, strip_u)
    views = (
        tiles.at[:, :, edge:],
        tiles.at[:, :, :STRIP],
        tiles.at[:, edge:, :],
        tiles.at[:, :STRIP, :],
    )
    loads = [pltpu.make_async_copy(v, s, load_sem.at[k]) for k, (v, s) in enumerate(zip(views, own))]
    for load in loads:
        load.start()

    pl.semaphore_wait(barrier, 6)

    def send(index, src, dst, place):
        copy = pltpu.make_async_remote_copy(
            src_ref=src,
            dst_ref=dst,
            send_sem=send_sem.at[index],
            recv_sem=recv_sem.at[index],
            device_id=place,
            device_id_type=MESH,
        )
        copy.start()
        return copy

    bulk = [
        send(RIGHT_1, tiles.at[:, half:, edge:], half_l, four[0]),
        send(LEFT_1, tiles.at[:, :half, :STRIP], half_r, four[1]),
        send(DOWN_1, tiles.at[:, edge:, half:], half_u, four[2]),
        send(UP_1, tiles.at[:, :STRIP, :half], half_d, four[3]),
    ]

    ext = (
        extents[0, row, col],
        extents[0, row, left],
        extents[1, row, col],
        extents[1, up, col],
    )
    valid = (col < n_col - 1, col > 0, row < n_row - 1, row > 0)
    lanes = lax.broadcasted_iota(jnp.int32, (8, LANES), 1)
    masks = (lanes < ext[0], lanes < ext[1])
    numbers = [(e * tile).astype(F32) for e in ext]

    means, variances = [], []
    for side in range(4):
        loads[side].wait()
        ref = own[side]
        reduce = sum_tall if side < 2 else sum_wide
        window = masks[side] if side < 2 else ext[side]
        mean = rows_of([reduce(ref, p, window, lambda x: x) for p in range(PLANES)]) / numbers[side]

        def square(p):
            m = mean[p : p + 1, :]

            def term(x):
                d = x - (m if side < 2 else m[:, :1])
                return d * d

            return reduce(ref, p, window, term)

        var = rows_of([square(p) for p in range(PLANES)]) / numbers[side]
        means.append(mean)
        variances.append(var)
        stats_out[side, 0:2, :] = mean
        stats_out[side, 2:4, :] = var

    opposite = (1, 0, 3, 2)
    small = [send(STATS + s, stats_out.at[s], stats_in.at[opposite[s]], four[s]) for s in range(4)]
    for copy in small:
        copy.wait()
    far_means = [stats_in[s, 0:2, :] for s in range(4)]
    far_vars = [stats_in[s, 2:4, :] for s in range(4)]

    received = (half_r, half_l, half_d, half_u)
    starts = (0, half, 0, half)
    bulk[1].wait()
    bulk[0].wait()
    bulk.append(send(RIGHT_2, tiles.at[:, :half, edge:], left_in.at[:, :half, :], four[0]))
    bulk.append(send(CORNER, half_l.at[:, half - STRIP :, :], corner_in, four[2]))
    bulk[3].wait()
    bulk[2].wait()
    bulk.append(send(DOWN_2, tiles.at[:, edge:, :half], up_in.at[:, :, :half], four[2]))
    keep = [
        pltpu.make_async_copy(half_l, left_in.at[:, half:, :], load_sem.at[4]),
        pltpu.make_async_copy(half_u, up_in.at[:, :, half:], load_sem.at[5]),
    ]
    for copy in keep:
        copy.start()

    for side in range(4):
        function = cov_tall if side < 2 else cov_wide
        window = masks[side] if side < 2 else ext[side]
        cov_out[side, 0:2, :] = rows_of(
            [
                function(
                    own[side],
                    starts[side],
                    received[side],
                    means[side][p : p + 1, :],
                    far_means[side][p : p + 1, :],
                    p,
                    window,
                )
                for p in range(PLANES)
            ]
        )
    small = [send(COV + s, cov_out.at[s], cov_in.at[opposite[s]], four[s]) for s in range(4)]
    for copy in small:
        copy.wait()
    cov = [(cov_out[s, 0:2, :] + cov_in[s, 0:2, :]) / numbers[s] for s in range(4)]

    def tile_terms(near_means, near_vars, distant_means, distant_vars, covs):
        parts = []
        for s in range(4):
            near, far = (near_means[s], near_vars[s]), (distant_means[s], distant_vars[s])
            first, second = (near, far) if s in (0, 2) else (far, near)
            parts.append(pair_terms(*first, *second, covs[s], valid[s]))
        return combine(*parts)

    gain_one, level_one = tile_terms(means, variances, far_means, far_vars, cov)
    first_out[0:2, :] = gain_one
    first_out[2:4, :] = level_one
    small = [send(FIRST + s, first_out, first_in.at[opposite[s]], four[s]) for s in range(4)]
    scale = jnp.exp(gain_one)
    near_means = [scale * m + level_one for m in means]
    near_vars = [scale * (scale * v) for v in variances]
    for copy in small:
        copy.wait()
    far_scale = [jnp.exp(first_in[s, 0:2, :]) for s in range(4)]
    far_level = [first_in[s, 2:4, :] for s in range(4)]
    gain_two, level_two = tile_terms(
        near_means,
        near_vars,
        [far_scale[s] * far_means[s] + far_level[s] for s in range(4)],
        [far_scale[s] * (far_scale[s] * far_vars[s]) for s in range(4)],
        [scale * (far_scale[s] * cov[s]) for s in range(4)],
    )
    gain = jnp.exp(gain_one + gain_two)
    level = jnp.exp(gain_two) * level_one + level_two
    final_out[0:2, :] = gain
    final_out[2:4, :] = level
    small = [
        send(FINAL + k, final_out, final_in.at[k], place)
        for k, place in enumerate((four[0], four[2], diag))
    ]
    terms[0, 0:2, :] = gain
    terms[0, 2:4, :] = level
    for copy in small:
        copy.wait()
    for k in range(3):
        terms[k + 1, :, :] = final_in[k]
    for copy in bulk[4:]:
        copy.wait()
    for copy in keep:
        copy.wait()


def exchange(tiles, extents):
    planes, tile, _ = tiles.shape
    dtype = tiles.dtype
    half = tile // 2
    tall = pltpu.VMEM((planes, tile, STRIP), dtype)
    wide = pltpu.VMEM((planes, STRIP, tile), dtype)
    half_tall = pltpu.VMEM((planes, half, STRIP), dtype)
    half_wide = pltpu.VMEM((planes, STRIP, half), dtype)
    message = pltpu.VMEM((4, 4, LANES), F32)
    single = pltpu.VMEM((4, LANES), F32)
    any_space = pl.BlockSpec(memory_space=pl.ANY)
    return pl.pallas_call(
        exchange_kernel,
        name="exchange",
        out_shape=(
            jax.ShapeDtypeStruct((planes, tile, STRIP), dtype),
            jax.ShapeDtypeStruct((planes, STRIP, tile), dtype),
            jax.ShapeDtypeStruct((planes, STRIP, STRIP), dtype),
            jax.ShapeDtypeStruct((4, 4, LANES), F32),
        ),
        in_specs=[pl.BlockSpec(memory_space=pltpu.SMEM), any_space],
        out_specs=(any_space, any_space, any_space, pl.BlockSpec(memory_space=pltpu.VMEM)),
        scratch_shapes=[
            tall, tall, wide, wide, half_tall, half_tall, half_wide, half_wide,
            message, message, message, message, single, message, single, message,
            pltpu.SemaphoreType.DMA((6,)),
            pltpu.SemaphoreType.DMA((COPIES,)),
            pltpu.SemaphoreType.DMA((COPIES,)),
        ],
        compiler_params=pltpu.CompilerParams(
            collective_id=0, has_side_effects=True, vmem_limit_bytes=32 * 1024 * 1024
        ),
    )(extents, tiles)


def fade(ids, limit, tile):
    steps = jnp.minimum(ids, tile - 1 - ids) + 1
    return jnp.where(limit, steps.astype(F32) * (2.0 / tile), 0.0)


def blend_kernel(
    places, offsets, bands, tiles, left_in, up_in, corner_in, terms, blended, weights,
    raw, raw_left, raw_up, raw_corner, moved, moved_left, moved_up, moved_corner, sem,
):
    step = pl.program_id(0)
    tile = raw.shape[1]
    blocks = tile // LANES
    rows = weights.shape[0]
    lanes = lax.broadcasted_iota(jnp.int32, (rows, LANES), 1)
    lines = lax.broadcasted_iota(jnp.int32, (rows, LANES), 0)
    row, col = places[0], places[1]
    up, left = jnp.maximum(row - 1, 0), jnp.maximum(col - 1, 0)

    def settings(r, c):
        return offsets[0, r, c], offsets[1, r, c], bands[0, r, c] * BLOCK, bands[1, r, c] * BLOCK

    def piece(k):
        part = pl.ds(pl.multiple_of(k * rows, rows), rows)
        return pltpu.make_async_copy(tiles.at[:, part, :], raw.at[:, part, :], sem.at[k])

    others = [
        pltpu.make_async_copy(src, dst, sem.at[blocks + k])
        for k, (src, dst) in enumerate(
            ((left_in, raw_left), (up_in, raw_up), (corner_in, raw_corner))
        )
    ]

    @pl.when(step == 0)
    def _():
        piece(0).start()
        for copy in others:
            copy.start()
        for k in range(1, tile // rows):
            piece(k).start()
        moved[:, :, 0:SPILL, :] = jnp.zeros((PLANES, blocks, SPILL, LANES), F32)
        moved_left[:, 0:SPILL, :] = jnp.zeros((PLANES, SPILL, LANES), F32)
        moved_up[:, :, SPILL:, :] = jnp.zeros((PLANES, blocks, SPILL, LANES), F32)
        moved_corner[:, SPILL:, :] = jnp.zeros((PLANES, SPILL, LANES), F32)
        for copy in others:
            copy.wait()

    piece(step).wait()
    first = pl.multiple_of(step * rows, rows)

    def shifted(load, shift, store):
        before = None
        for v in range(blocks):
            now = pltpu.roll(load(v).astype(F32), shift, 1)
            store(v, now if before is None else jnp.where(lanes < shift, before, now))
            before = now

    dy, dx, low, high = settings(row, col)
    here = pl.ds(first, rows)
    there = pl.ds(pl.multiple_of(first + SPILL, SPILL), rows)
    for p in range(PLANES):

        def store(v, x):
            moved[p, v, there, :] = x

        shifted(lambda v: raw[p, here, v * LANES : (v + 1) * LANES], dx, store)

    i = lines + (first - dy)
    row_fade = fade(i, (i >= jnp.maximum(low, 0)) & (i < high), tile)
    source = pl.ds(first + SPILL - dy, rows)
    for v in range(blocks):
        j = lanes + (v * LANES - dx)
        weight = row_fade * fade(j, j >= 0, tile)
        weights[:, v * LANES : (v + 1) * LANES] = weight
        for p in range(PLANES):
            x = moved[p, v, source, :]
            gain, level = terms[0, p : p + 1, :], terms[0, 2 + p : 3 + p, :]
            blended[p, :, v * LANES : (v + 1) * LANES] = (gain * x + level) * weight

    dy, dx, low, high = settings(row, left)
    for p in range(PLANES):
        moved_left[p, there, :] = pltpu.roll(raw_left[p, here, :].astype(F32), dx, 1)
    i = lines + (first - dy)
    j = lanes + (tile - dx)
    weight = fade(i, (i >= jnp.maximum(low, 0)) & (i < high) & (col > 0), tile)
    weight = weight * fade(j, j < tile, tile)
    source = pl.ds(first + SPILL - dy, rows)
    weights[:, 0:LANES] += weight
    for p in range(PLANES):
        x = moved_left[p, source, :]
        gain, level = terms[1, p : p + 1, :], terms[1, 2 + p : 3 + p, :]
        blended[p, :, 0:LANES] += (gain * x + level) * weight

    @pl.when((step == 0) & (row > 0))
    def _():
        dy, dx, low, high = settings(up, col)
        for p in range(PLANES):

            def store(v, x):
                moved_up[p, v, 0:SPILL, :] = x

            shifted(lambda v: raw_up[p, :, v * LANES : (v + 1) * LANES], dx, store)
        i = lines + (tile - dy)
        row_fade = fade(i, (i >= low) & (i < jnp.minimum(high, tile)), tile)
        source = pl.ds(SPILL - dy, rows)
        for v in range(blocks):
            j = lanes + (v * LANES - dx)
            weight = row_fade * fade(j, j >= 0, tile)
            weights[:, v * LANES : (v + 1) * LANES] += weight
            for p in range(PLANES):
                x = moved_up[p, v, source, :]
                gain, level = terms[2, p : p + 1, :], terms[2, 2 + p : 3 + p, :]
                blended[p, :, v * LANES : (v + 1) * LANES] += (gain * x + level) * weight

        @pl.when(col > 0)
        def _():
            dy, dx, low, high = settings(up, left)
            for p in range(PLANES):
                moved_corner[p, 0:SPILL, :] = pltpu.roll(raw_corner[p].astype(F32), dx, 1)
            i = lines + (tile - dy)
            j = lanes + (tile - dx)
            weight = fade(i, (i >= low) & (i < jnp.minimum(high, tile)), tile)
            weight = weight * fade(j, j < tile, tile)
            source = pl.ds(SPILL - dy, rows)
            weights[:, 0:LANES] += weight
            for p in range(PLANES):
                x = moved_corner[p, source, :]
                gain, level = terms[3, p : p + 1, :], terms[3, 2 + p : 3 + p, :]
                blended[p, :, 0:LANES] += (gain * x + level) * weight


def blend(tiles, offsets, bands, left_in, up_in, corner_in, terms):
    planes, tile, _ = tiles.shape
    dtype = tiles.dtype
    rows = BLOCK
    blocks = tile // LANES
    any_space = pl.BlockSpec(memory_space=pl.ANY)
    small = pl.BlockSpec(memory_space=pltpu.SMEM)
    places = jnp.stack([lax.axis_index("row"), lax.axis_index("col")]).astype(jnp.int32)
    return pl.pallas_call(
        blend_kernel,
        name="blend",
        grid=(tile // rows,),
        out_shape=(
            jax.ShapeDtypeStruct((planes, tile, tile), F32),
            jax.ShapeDtypeStruct((tile, tile), F32),
        ),
        in_specs=[small, small, small, any_space, any_space, any_space, any_space,
                  pl.BlockSpec(memory_space=pltpu.VMEM)],
        out_specs=(
            pl.BlockSpec((planes, rows, tile), lambda i: (0, i, 0)),
            pl.BlockSpec((rows, tile), lambda i: (i, 0)),
        ),
        scratch_shapes=[
            pltpu.VMEM((planes, tile, tile), dtype),
            pltpu.VMEM((planes, tile, STRIP), dtype),
            pltpu.VMEM((planes, STRIP, tile), dtype),
            pltpu.VMEM((planes, STRIP, STRIP), dtype),
            pltpu.VMEM((planes, blocks, SPILL + tile, LANES), F32),
            pltpu.VMEM((planes, SPILL + tile, LANES), F32),
            pltpu.VMEM((planes, blocks, 2 * SPILL, LANES), F32),
            pltpu.VMEM((planes, 2 * SPILL, LANES), F32),
            pltpu.SemaphoreType.DMA((tile // rows + 3,)),
        ],
        compiler_params=pltpu.CompilerParams(vmem_limit_bytes=48 * 1024 * 1024),
    )(places, offsets, bands, tiles, left_in, up_in, corner_in, terms)


def local(tiles, extents, offsets, bands):
    left_in, up_in, corner_in, terms = exchange(tiles, extents)
    return blend(tiles, offsets, bands, left_in, up_in, corner_in, terms)


def solution(mesh):
    return jax.shard_map(
        local,
        mesh=mesh,
        in_specs=(P(None, "row", "col"), P(), P(), P()),
        out_specs=(P(None, "row", "col"), P("row", "col")),
        check_vma=False,
    )
```

```python
import jax
import jax.numpy as jnp
from jax import lax
from jax.experimental import pallas as pl
from jax.experimental.pallas import tpu as pltpu
from jax.sharding import PartitionSpec as P

STRIP = 128
SPILL = 128
BLOCK = 128
LANES = 128
PLANES = 2
EPS = 1e-6
MESH = pl.DeviceIdType.MESH
F32 = jnp.float32

CENTRE = 36
BLENDED = ((0, 0), (0, -1), (-1, 0), (-1, -1))
SOURCES = tuple(
    (r, c)
    for r in range(-3, 3)
    for c in range(-3, 3)
    if min(abs(r - a) + abs(c - b) for a, b in BLENDED) <= 2 and (r, c) != (0, 0)
)
RIGHT_1, LEFT_1, DOWN_1, UP_1, RIGHT_2, DOWN_2, CORNER = range(7)


def slot_of(r, c):
    return CENTRE + 8 * r + c


def total(x):
    return jnp.sum(x, keepdims=True)


def fold(x):
    return jnp.sum(x.reshape(x.shape[0] // 8, 8, x.shape[1]), axis=0)


def sum_tall(ref, plane, first, mask, term):
    size = 128

    def body(i, acc):
        part = pl.ds(pl.multiple_of(i * size, size), size)
        x = ref[plane, part, first : first + STRIP].astype(F32)
        return acc + fold(term(x))

    acc = lax.fori_loop(0, ref.shape[1] // size, body, jnp.zeros((8, LANES), F32))
    return total(jnp.where(mask, acc, 0.0))


def sum_wide(ref, plane, first, extent, term):
    size = 16
    ids = lax.broadcasted_iota(jnp.int32, (size, LANES), 0)

    def body(i, acc):
        x = ref[plane, pl.ds(pl.multiple_of(first + i * size, size), size), :].astype(F32)
        t = term(x)
        part = sum(t[:, k : k + LANES] for k in range(0, x.shape[1], LANES))
        return acc + fold(jnp.where(ids + i * size < extent, part, 0.0))

    return total(lax.fori_loop(0, STRIP // size, body, jnp.zeros((8, LANES), F32)))


def cov_tall(own, row, col, other, other_row, count, means, plane, mask):
    size = 128

    def body(i, acc):
        start = pl.multiple_of(i * size, size)
        x = own[plane, pl.ds(row + start, size), col : col + STRIP].astype(F32) - means[0]
        y = other[plane, pl.ds(other_row + start, size), :].astype(F32) - means[1]
        return acc + fold(x * y)

    acc = lax.fori_loop(0, count // size, body, jnp.zeros((8, LANES), F32))
    return total(jnp.where(mask, acc, 0.0))


def cov_wide(own, row, col, other, other_col, count, means, plane, extent):
    size = 16
    ids = lax.broadcasted_iota(jnp.int32, (size, LANES), 0)

    def body(i, acc):
        start = pl.multiple_of(i * size, size)
        x = own[plane, pl.ds(row + start, size), col : col + count].astype(F32) - means[0]
        y = other[plane, pl.ds(start, size), other_col : other_col + count].astype(F32) - means[1]
        t = x * y
        part = sum(t[:, k : k + LANES] for k in range(0, count, LANES))
        return acc + fold(jnp.where(ids + i * size < extent, part, 0.0))

    return total(lax.fori_loop(0, STRIP // size, body, jnp.zeros((8, LANES), F32)))


def pair_terms(mean_a, var_a, mean_b, var_b, cov, valid):
    weight = cov * cov / ((var_a + EPS) * (var_b + EPS))
    ratio = 0.25 * (jnp.log(var_b + EPS) - jnp.log(var_a + EPS))
    shift = 0.5 * (mean_b - mean_a)
    return tuple(jnp.where(valid, t, 0.0) for t in (weight, weight * ratio, weight * shift))


def ahead(x, distance):
    return pltpu.roll(x, (LANES - distance) % LANES, 1)


def tile_terms(means, variances, covs, valid):
    across = pair_terms(means[0], variances[0], ahead(means[1], 1), ahead(variances[1], 1), covs[0], valid[0])
    along = pair_terms(means[2], variances[2], ahead(means[3], 8), ahead(variances[3], 8), covs[1], valid[1])
    back = [ahead(t, -1) for t in across]
    above = [ahead(t, -8) for t in along]
    scale = 1.0 + across[0] + along[0] + back[0] + above[0]
    return tuple((across[k] + along[k] - back[k] - above[k]) / scale for k in (1, 2))


def exchange_kernel(
    extents_in, offsets_in, tiles, shifted, left_in, up_in, corner_in, terms,
    extents, offsets, raw, half_r, half_d, moved, stats_out, stats_in, sums_out, sums_in,
    load_sem, send_sem, recv_sem, mean_send, mean_recv, sums_send, sums_recv,
):
    n_col, n_row = lax.axis_size("col"), lax.axis_size("row")
    col, row = lax.axis_index("col"), lax.axis_index("row")
    tile = raw.shape[1]
    half = tile // 2
    edge = tile - STRIP
    blocks = tile // LANES
    four = ((0, 1), (0, -1), (1, 0), (-1, 0))

    def exists(r, c):
        return (row + r >= 0) & (row + r < n_row) & (col + c >= 0) & (col + c < n_col)

    def place(r, c):
        return {"row": row + r, "col": col + c}

    sums_in[...] = jnp.zeros_like(sums_in)
    stats_in[...] = jnp.zeros_like(stats_in)

    barrier = pltpu.get_barrier_semaphore()
    expected = 0
    for r, c in SOURCES:

        @pl.when(exists(r, c))
        def _(r=r, c=c):
            pl.semaphore_signal(barrier, inc=1, device_id=place(r, c), device_id_type=MESH)

        expected = expected + exists(-r, -c).astype(jnp.int32)

    settings = [
        pltpu.make_async_copy(extents_in, extents, load_sem.at[blocks]),
        pltpu.make_async_copy(offsets_in, offsets, load_sem.at[blocks + 1]),
    ]
    for copy in settings:
        copy.start()
    loads = []
    for k in range(blocks):
        part = pl.ds(k * BLOCK, BLOCK)
        loads.append(pltpu.make_async_copy(tiles.at[:, part, :], raw.at[:, part, :], load_sem.at[k]))
        loads[k].start()

    pl.semaphore_wait(barrier, expected)

    class Remote:
        def __init__(self, src, dst, send, recv, r, c):
            self.there, self.here = exists(r, c), exists(-r, -c)
            self.copy = pltpu.make_async_remote_copy(
                src_ref=src,
                dst_ref=dst,
                send_sem=send,
                recv_sem=recv,
                device_id=place(r, c),
                device_id_type=MESH,
            )

        def start(self):
            pl.when(self.there)(self.copy.start)

        def wait_recv(self):
            pl.when(self.here)(self.copy.wait_recv)

        def wait_send(self):
            pl.when(self.there)(self.copy.wait_send)

    def bulk(index, src, dst, r, c):
        copy = Remote(src, dst, send_sem.at[index], recv_sem.at[index], r, c)
        copy.start()
        return copy

    first = [
        bulk(RIGHT_1, tiles.at[:, half:, edge:], left_in.at[:, half:, :], 0, 1),
        bulk(LEFT_1, tiles.at[:, :half, :STRIP], half_r, 0, -1),
        bulk(DOWN_1, tiles.at[:, edge:, half:], up_in.at[:, :, half:], 1, 0),
        bulk(UP_1, tiles.at[:, :STRIP, :half], half_d, -1, 0),
    ]

    for copy in settings:
        copy.wait()
    ext = (
        extents[0, row, col],
        extents[0, row, jnp.maximum(col - 1, 0)],
        extents[1, row, col],
        extents[1, jnp.maximum(row - 1, 0), col],
    )
    lanes = lax.broadcasted_iota(jnp.int32, (8, LANES), 1)
    windows = (lanes < ext[0], lanes < ext[1], ext[2], ext[3])
    numbers = [(e * tile).astype(F32) for e in ext]
    one = lax.broadcasted_iota(jnp.int32, (1, LANES), 1)

    for load in loads:
        load.wait()

    means = []
    packed = jnp.zeros((1, LANES), F32)
    for side in range(4):
        reduce = sum_tall if side < 2 else sum_wide
        begin = edge if side in (0, 2) else 0
        own_means = []
        for p in range(PLANES):
            mean = reduce(raw, p, begin, windows[side], lambda x: x) / numbers[side]

            def square(x, mean=mean):
                return (x - mean) * (x - mean)

            var = reduce(raw, p, begin, windows[side], square) / numbers[side]
            packed = jnp.where(one == 64 * p + 3 * side, mean, packed)
            packed = jnp.where(one == 64 * p + 3 * side + 1, var, packed)
            own_means.append(mean)
        means.append(own_means)
    stats_out[...] = packed
    opposite = (1, 0, 3, 2)
    early = []
    for side, (r, c) in enumerate(four):
        early.append(
            Remote(stats_out, stats_in.at[opposite[side]], mean_send.at[side], mean_recv.at[opposite[side]], r, c)
        )
        early[side].start()

    dy, dx = offsets[0, row, col], offsets[1, row, col]
    wide = lax.broadcasted_iota(jnp.int32, (BLOCK, LANES), 1)

    def shift_plane(p):
        moved[:, 0:SPILL, :] = jnp.zeros((blocks, SPILL, LANES), F32)

        def sideways(k, carry):
            start = pl.multiple_of(k * BLOCK, BLOCK)
            before = None
            for v in range(blocks):
                x = raw[p, pl.ds(start, BLOCK), v * LANES : (v + 1) * LANES].astype(F32)
                now = pltpu.roll(x, dx, 1)
                out = now if before is None else jnp.where(wide < dx, before, now)
                moved[v, pl.ds(start + SPILL, BLOCK), :] = out
                before = now
            return carry

        lax.fori_loop(0, blocks, sideways, 0)

        def downwards(k, carry):
            start = pl.multiple_of(k * BLOCK, BLOCK)
            for v in range(blocks):
                x = moved[v, pl.ds(start + SPILL - dy, BLOCK), :]
                shifted[p, pl.ds(start, BLOCK), v * LANES : (v + 1) * LANES] = x.astype(shifted.dtype)
            return carry

        lax.fori_loop(0, blocks, downwards, 0)

    shift_plane(0)

    for copy in early:
        copy.wait_recv()

    first[0].wait_recv()
    first[1].wait_recv()
    first[2].wait_recv()
    first[3].wait_recv()
    for side in range(4):
        far = stats_in[side]
        for p in range(PLANES):
            k = 64 * p + 3 * opposite[side]
            pair = (means[side][p], far[:, k : k + 1])
            if side == 0:
                cov = cov_tall(raw, 0, edge, half_r, 0, half, pair, p, windows[side])
            elif side == 1:
                cov = cov_tall(raw, half, 0, left_in, half, half, pair, p, windows[side])
            elif side == 2:
                cov = cov_wide(raw, edge, 0, half_d, 0, half, pair, p, windows[side])
            else:
                cov = cov_wide(raw, 0, half, up_in, half, half, pair, p, windows[side])
            packed = jnp.where(one == 64 * p + 3 * side + 2, cov / numbers[side], packed)
    sums_out[...] = packed
    sums_in[CENTRE] = packed
    spread = []
    for k, (r, c) in enumerate(SOURCES):
        copy = Remote(sums_out, sums_in.at[slot_of(r, c)], sums_send.at[k], sums_recv.at[k], -r, -c)
        copy.start()
        spread.append(copy)

    second = [
        bulk(RIGHT_2, tiles.at[:, :half, edge:], left_in.at[:, :half, :], 0, 1),
        bulk(DOWN_2, tiles.at[:, edge:, :half], up_in.at[:, :, :half], 1, 0),
        bulk(CORNER, left_in.at[:, edge:, :], corner_in, 1, 0),
    ]

    shift_plane(1)

    for copy in spread:
        copy.wait_recv()

    table = jnp.transpose(sums_in[:, 0, :])

    def quantity(k):
        return jnp.concatenate([table[k : k + 1, :], table[64 + k : 65 + k, :]], axis=0)

    slot = lax.broadcasted_iota(jnp.int32, (PLANES, LANES), 1)
    slot_row = row + lax.shift_right_logical(slot, 3) - 4
    slot_col = col + (slot & 7) - 4
    inside = (slot_row >= 0) & (slot_row < n_row) & (slot_col >= 0) & (slot_col < n_col)
    valid = (inside & (slot_col < n_col - 1), inside & (slot_row < n_row - 1))
    sides = [quantity(3 * side) for side in range(4)]
    spreads = [quantity(3 * side + 1) for side in range(4)]
    covs = (quantity(2) + ahead(quantity(5), 1), quantity(8) + ahead(quantity(11), 8))
    gain_one, level_one = tile_terms(sides, spreads, covs, valid)
    scale = jnp.exp(gain_one)
    gain_two, level_two = tile_terms(
        [scale * m + level_one for m in sides],
        [scale * (scale * v) for v in spreads],
        (scale * (ahead(scale, 1) * covs[0]), scale * (ahead(scale, 8) * covs[1])),
        valid,
    )
    gain = jnp.exp(gain_one + gain_two)
    level = jnp.exp(gain_two) * level_one + level_two
    for k, (r, c) in enumerate(BLENDED):
        s = slot_of(r, c)
        terms[k, 0:2, :] = jnp.broadcast_to(gain[:, s : s + 1], (PLANES, LANES))
        terms[k, 2:4, :] = jnp.broadcast_to(level[:, s : s + 1], (PLANES, LANES))
    for copy in second:
        copy.wait_recv()
    for copy in (*early, *first, *spread, *second):
        copy.wait_send()


def exchange(tiles, extents, offsets):
    planes, tile, _ = tiles.shape
    dtype = tiles.dtype
    half = tile // 2
    blocks = tile // LANES
    in_vmem = pl.BlockSpec(memory_space=pltpu.VMEM)
    one = pltpu.VMEM((1, LANES), F32)
    dma = pltpu.SemaphoreType.DMA
    return pl.pallas_call(
        exchange_kernel,
        name="exchange",
        out_shape=(
            jax.ShapeDtypeStruct((planes, tile, tile), dtype),
            jax.ShapeDtypeStruct((planes, tile, STRIP), dtype),
            jax.ShapeDtypeStruct((planes, STRIP, tile), dtype),
            jax.ShapeDtypeStruct((planes, STRIP, STRIP), dtype),
            jax.ShapeDtypeStruct((4, 4, LANES), F32),
        ),
        in_specs=[pl.BlockSpec(memory_space=pl.ANY)] * 3,
        out_specs=(in_vmem,) * 5,
        scratch_shapes=[
            pltpu.SMEM(extents.shape, extents.dtype),
            pltpu.SMEM(offsets.shape, offsets.dtype),
            pltpu.VMEM((planes, tile, tile), dtype),
            pltpu.VMEM((planes, half, STRIP), dtype),
            pltpu.VMEM((planes, STRIP, half), dtype),
            pltpu.VMEM((blocks, SPILL + tile, LANES), F32),
            one,
            pltpu.VMEM((4, 1, LANES), F32),
            one,
            pltpu.VMEM((LANES, 1, LANES), F32),
            dma((blocks + 2,)),
            dma((7,)),
            dma((7,)),
            dma((4,)),
            dma((4,)),
            dma((len(SOURCES),)),
            dma((len(SOURCES),)),
        ],
        compiler_params=pltpu.CompilerParams(
            collective_id=0, has_side_effects=True, vmem_limit_bytes=48 * 1024 * 1024
        ),
    )(extents, offsets, tiles)


def fade(ids, limit, tile):
    steps = jnp.minimum(ids, tile - 1 - ids) + 1
    return jnp.where(limit, steps.astype(F32) * (2.0 / tile), 0.0)


def blend_kernel(
    places, offsets, bands, shifted, raw_left, raw_up, raw_corner, terms, blended, weights,
    moved_left, moved_up, moved_corner,
):
    step = pl.program_id(0)
    rows = weights.shape[0]
    tile = weights.shape[1]
    blocks = tile // LANES
    lanes = lax.broadcasted_iota(jnp.int32, (rows, LANES), 1)
    lines = lax.broadcasted_iota(jnp.int32, (rows, LANES), 0)
    row, col = places[0], places[1]
    up, left = jnp.maximum(row - 1, 0), jnp.maximum(col - 1, 0)
    block = lax.rem(step + 1, tile // rows)
    first = pl.multiple_of(block * rows, rows)
    here = pl.ds(first, rows)

    def settings(r, c):
        return offsets[0, r, c], offsets[1, r, c], bands[0, r, c] * BLOCK, bands[1, r, c] * BLOCK

    def corrected(x, k, p):
        return terms[k, p : p + 1, :] * x + terms[k, 2 + p : 3 + p, :]

    @pl.when(step == 0)
    def _():
        moved_left[:, 0:SPILL, :] = jnp.zeros((PLANES, SPILL, LANES), F32)
        dx = offsets[1, row, left]
        for k in range(blocks):
            for p in range(PLANES):
                x = raw_left[p, k * BLOCK : (k + 1) * BLOCK, :].astype(F32)
                moved_left[p, SPILL + k * BLOCK : SPILL + (k + 1) * BLOCK, :] = pltpu.roll(x, dx, 1)

    dy, dx, low, high = settings(row, col)
    i = lines + (first - dy)
    row_fade = fade(i, (i >= jnp.maximum(low, 0)) & (i < high), tile)
    for v in range(blocks):
        j = lanes + (v * LANES - dx)
        weight = row_fade * fade(j, j >= 0, tile)
        weights[:, v * LANES : (v + 1) * LANES] = weight
        for p in range(PLANES):
            x = shifted[p, here, v * LANES : (v + 1) * LANES].astype(F32)
            blended[p, :, v * LANES : (v + 1) * LANES] = corrected(x, 0, p) * weight

    @pl.when(col > 0)
    def _():
        dy, dx, low, high = settings(row, left)
        i = lines + (first - dy)
        j = lanes + (tile - dx)
        weight = fade(i, (i >= jnp.maximum(low, 0)) & (i < high), tile) * fade(j, j < tile, tile)
        source = pl.ds(first + SPILL - dy, rows)
        weights[:, 0:LANES] += weight
        for p in range(PLANES):
            blended[p, :, 0:LANES] += corrected(moved_left[p, source, :], 1, p) * weight

    @pl.when((block == 0) & (row > 0))
    def _():
        dy, dx, low, high = settings(up, col)
        for p in range(PLANES):
            before = None
            for v in range(blocks):
                now = pltpu.roll(raw_up[p, :, v * LANES : (v + 1) * LANES].astype(F32), dx, 1)
                moved_up[p, v, 0:SPILL, :] = now if before is None else jnp.where(lanes < dx, before, now)
                moved_up[p, v, SPILL:, :] = jnp.zeros((SPILL, LANES), F32)
                before = now
        i = lines + (tile - dy)
        row_fade = fade(i, (i >= low) & (i < jnp.minimum(high, tile)), tile)
        source = pl.ds(SPILL - dy, rows)
        for v in range(blocks):
            j = lanes + (v * LANES - dx)
            weight = row_fade * fade(j, j >= 0, tile)
            weights[:, v * LANES : (v + 1) * LANES] += weight
            for p in range(PLANES):
                x = moved_up[p, v, source, :]
                blended[p, :, v * LANES : (v + 1) * LANES] += corrected(x, 2, p) * weight

        @pl.when(col > 0)
        def _():
            dy, dx, low, high = settings(up, left)
            for p in range(PLANES):
                moved_corner[p, 0:SPILL, :] = pltpu.roll(raw_corner[p].astype(F32), dx, 1)
                moved_corner[p, SPILL:, :] = jnp.zeros((SPILL, LANES), F32)
            i = lines + (tile - dy)
            j = lanes + (tile - dx)
            weight = fade(i, (i >= low) & (i < jnp.minimum(high, tile)), tile) * fade(j, j < tile, tile)
            source = pl.ds(SPILL - dy, rows)
            weights[:, 0:LANES] += weight
            for p in range(PLANES):
                blended[p, :, 0:LANES] += corrected(moved_corner[p, source, :], 3, p) * weight


def blend(offsets, bands, shifted, left_in, up_in, corner_in, terms):
    planes, tile, _ = shifted.shape
    rows = BLOCK
    blocks = tile // LANES
    count = tile // rows
    in_vmem = pl.BlockSpec(memory_space=pltpu.VMEM)
    in_smem = pl.BlockSpec(memory_space=pltpu.SMEM)
    places = jnp.stack([lax.axis_index("row"), lax.axis_index("col")]).astype(jnp.int32)
    return pl.pallas_call(
        blend_kernel,
        name="blend",
        grid=(count,),
        out_shape=(
            jax.ShapeDtypeStruct((planes, tile, tile), F32),
            jax.ShapeDtypeStruct((tile, tile), F32),
        ),
        in_specs=[in_smem] * 3 + [in_vmem] * 5,
        out_specs=(
            pl.BlockSpec((planes, rows, tile), lambda i: (0, lax.rem(i + 1, count), 0)),
            pl.BlockSpec((rows, tile), lambda i: (lax.rem(i + 1, count), 0)),
        ),
        scratch_shapes=[
            pltpu.VMEM((planes, SPILL + tile, LANES), F32),
            pltpu.VMEM((planes, blocks, 2 * SPILL, LANES), F32),
            pltpu.VMEM((planes, 2 * SPILL, LANES), F32),
        ],
        compiler_params=pltpu.CompilerParams(vmem_limit_bytes=32 * 1024 * 1024),
    )(places, offsets, bands, shifted, left_in, up_in, corner_in, terms)


def local(tiles, extents, offsets, bands):
    shifted, left_in, up_in, corner_in, terms = exchange(tiles, extents, offsets)
    return blend(offsets, bands, shifted, left_in, up_in, corner_in, terms)


def solution(mesh):
    return jax.shard_map(
        local,
        mesh=mesh,
        in_specs=(P(None, "row", "col"), P(), P(), P()),
        out_specs=(P(None, "row", "col"), P("row", "col")),
        check_vma=False,
    )
```

```python
import jax
import jax.numpy as jnp
from jax import lax
from jax.experimental import pallas as pl
from jax.experimental.pallas import tpu as pltpu
from jax.sharding import PartitionSpec as P

STRIP = 128
SPILL = 128
BLOCK = 128
LANES = 128
ROWS = 64
PLANES = 2
EPS = 1e-6
MESH = pl.DeviceIdType.MESH
F32 = jnp.float32

CENTRE = 36
BLENDED = ((0, 0), (0, -1), (-1, 0), (-1, -1))
SOURCES = tuple(
    (r, c)
    for r in range(-3, 3)
    for c in range(-3, 3)
    if min(abs(r - a) + abs(c - b) for a, b in BLENDED) <= 2 and (r, c) != (0, 0)
)
RIGHT_1, LEFT_1, DOWN_1, UP_1, RIGHT_2, DOWN_2, CORNER = range(7)


def slot_of(r, c):
    return CENTRE + 8 * r + c


def total(x):
    return jnp.sum(x, keepdims=True)


def fold(x):
    return jnp.sum(x.reshape(x.shape[0] // 8, 8, x.shape[1]), axis=0)


def sum_tall(ref, plane, first, mask, term):
    size = 128

    def body(i, acc):
        part = pl.ds(pl.multiple_of(i * size, size), size)
        x = ref[plane, part, first : first + STRIP].astype(F32)
        return acc + fold(term(x))

    acc = lax.fori_loop(0, ref.shape[1] // size, body, jnp.zeros((8, LANES), F32))
    return total(jnp.where(mask, acc, 0.0))


def sum_wide(ref, plane, first, extent, term):
    size = 16
    ids = lax.broadcasted_iota(jnp.int32, (size, LANES), 0)

    def body(i, acc):
        x = ref[plane, pl.ds(pl.multiple_of(first + i * size, size), size), :].astype(F32)
        t = term(x)
        part = sum(t[:, k : k + LANES] for k in range(0, x.shape[1], LANES))
        return acc + fold(jnp.where(ids + i * size < extent, part, 0.0))

    return total(lax.fori_loop(0, STRIP // size, body, jnp.zeros((8, LANES), F32)))


def cov_tall(own, row, col, other, other_row, count, means, plane, mask):
    size = 128
    acc = jnp.zeros((8, LANES), F32)
    for start in range(0, count, size):
        x = own[plane, row + start : row + start + size, col : col + STRIP].astype(F32)
        y = other[plane, other_row + start : other_row + start + size, :].astype(F32)
        x = x.reshape(size // 8, 8, LANES) - means[0][None]
        y = y.reshape(size // 8, 8, LANES) - means[1][None]
        acc = acc + jnp.sum(x * y, axis=0)
    return jnp.sum(jnp.where(mask, acc, 0.0), axis=0, keepdims=True)


def cov_wide(own, row, col, other, other_col, count, means, plane, extent):
    size = 16
    ids = lax.broadcasted_iota(jnp.int32, (8, LANES), 0)
    acc = jnp.zeros((8, LANES), F32)
    for start in range(0, STRIP, size):
        part = jnp.zeros((size // 8, 8, LANES), F32)
        for k in range(0, count, LANES):
            x = own[plane, row + start : row + start + size, col + k : col + k + LANES].astype(F32)
            y = other[plane, start : start + size, other_col + k : other_col + k + LANES].astype(F32)
            x = x.reshape(size // 8, 8, LANES) - means[0][None]
            y = y.reshape(size // 8, 8, LANES) - means[1][None]
            part = part + x * y
        for k in range(size // 8):
            acc = acc + jnp.where(ids + (start + 8 * k) < extent, part[k], 0.0)
    return jnp.sum(acc, axis=0, keepdims=True)


def pair_terms(mean_a, var_a, mean_b, var_b, cov, valid):
    weight = cov * cov / ((var_a + EPS) * (var_b + EPS))
    ratio = 0.25 * (jnp.log(var_b + EPS) - jnp.log(var_a + EPS))
    shift = 0.5 * (mean_b - mean_a)
    return tuple(jnp.where(valid, t, 0.0) for t in (weight, weight * ratio, weight * shift))


def ahead(x, distance):
    return pltpu.roll(x, (LANES - distance) % LANES, 1)


def tile_terms(means, variances, covs, valid):
    across = pair_terms(means[0], variances[0], ahead(means[1], 1), ahead(variances[1], 1), covs[0], valid[0])
    along = pair_terms(means[2], variances[2], ahead(means[3], 8), ahead(variances[3], 8), covs[1], valid[1])
    back = [ahead(t, -1) for t in across]
    above = [ahead(t, -8) for t in along]
    scale = 1.0 + across[0] + along[0] + back[0] + above[0]
    return tuple((across[k] + along[k] - back[k] - above[k]) / scale for k in (1, 2))


def exchange_kernel(
    settings_in, tiles, shifted, left_in, up_in, corner_in, terms, places,
    settings, raw, half_r, half_d, moved, stats_out, stats_in, sums_out, sums_in,
    load_sem, send_sem, recv_sem, mean_send, mean_recv, sums_send, sums_recv,
):
    n_col, n_row = lax.axis_size("col"), lax.axis_size("row")
    col, row = lax.axis_index("col"), lax.axis_index("row")
    tile = raw.shape[1]
    half = tile // 2
    edge = tile - STRIP
    blocks = tile // LANES
    four = ((0, 1), (0, -1), (1, 0), (-1, 0))

    def exists(r, c):
        return (row + r >= 0) & (row + r < n_row) & (col + c >= 0) & (col + c < n_col)

    def place(r, c):
        return {"row": row + r, "col": col + c}

    sums_in[...] = jnp.zeros_like(sums_in)
    stats_in[...] = jnp.zeros_like(stats_in)

    barrier = pltpu.get_barrier_semaphore()
    expected = 0
    for r, c in SOURCES:

        @pl.when(exists(r, c))
        def _(r=r, c=c):
            pl.semaphore_signal(barrier, inc=1, device_id=place(r, c), device_id_type=MESH)

        expected = expected + exists(-r, -c).astype(jnp.int32)

    fetch = pltpu.make_async_copy(settings_in, settings, load_sem.at[blocks])
    fetch.start()
    loads = []
    for k in range(blocks):
        part = pl.ds(k * BLOCK, BLOCK)
        loads.append(pltpu.make_async_copy(tiles.at[:, part, :], raw.at[:, part, :], load_sem.at[k]))
        loads[k].start()

    pl.semaphore_wait(barrier, expected)

    class Remote:
        def __init__(self, src, dst, send, recv, r, c, wanted=True):
            self.there, self.here = exists(r, c) & wanted, exists(-r, -c) & wanted
            self.copy = pltpu.make_async_remote_copy(
                src_ref=src,
                dst_ref=dst,
                send_sem=send,
                recv_sem=recv,
                device_id=place(r, c),
                device_id_type=MESH,
            )

        def start(self):
            pl.when(self.there)(self.copy.start)

        def wait_recv(self):
            pl.when(self.here)(self.copy.wait_recv)

        def wait_send(self):
            pl.when(self.there)(self.copy.wait_send)

    def bulk(index, src, dst, r, c, wanted=True):
        copy = Remote(src, dst, send_sem.at[index], recv_sem.at[index], r, c, wanted)
        copy.start()
        return copy

    first = [
        bulk(RIGHT_1, tiles.at[:, half:, edge:], left_in.at[:, half:, :], 0, 1),
        bulk(LEFT_1, tiles.at[:, :half, :STRIP], half_r, 0, -1),
        bulk(DOWN_1, tiles.at[:, edge:, half:], up_in.at[:, :, half:], 1, 0),
        bulk(UP_1, tiles.at[:, :STRIP, :half], half_d, -1, 0),
    ]

    fetch.wait()
    ext = (
        settings[0, row, col],
        settings[0, row, jnp.maximum(col - 1, 0)],
        settings[1, row, col],
        settings[1, jnp.maximum(row - 1, 0), col],
    )
    lanes = lax.broadcasted_iota(jnp.int32, (8, LANES), 1)
    windows = (lanes < ext[0], lanes < ext[1], ext[2], ext[3])
    numbers = [(e * tile).astype(F32) for e in ext]
    one = lax.broadcasted_iota(jnp.int32, (1, LANES), 1)

    for load in loads:
        load.wait()

    means = []
    packed = jnp.zeros((1, LANES), F32)
    count_row = jnp.ones((1, LANES), F32)
    for side in range(4):
        reduce = sum_tall if side < 2 else sum_wide
        begin = edge if side in (0, 2) else 0
        own_means = []
        for p in range(PLANES):
            mean = reduce(raw, p, begin, windows[side], lambda x: x) / numbers[side]

            def square(x, mean=mean):
                return (x - mean) * (x - mean)

            var = reduce(raw, p, begin, windows[side], square) / numbers[side]
            packed = jnp.where(one == 64 * p + 3 * side, mean, packed)
            packed = jnp.where(one == 64 * p + 3 * side + 1, var, packed)
            count_row = jnp.where(one == 64 * p + 3 * side + 2, numbers[side], count_row)
            own_means.append(mean)
        means.append(own_means)
    stats_out[...] = packed
    opposite = (1, 0, 3, 2)
    early = []
    for side, (r, c) in enumerate(four):
        early.append(
            Remote(stats_out, stats_in.at[opposite[side]], mean_send.at[side], mean_recv.at[opposite[side]], r, c)
        )
        early[side].start()

    second = [bulk(RIGHT_2, tiles.at[:, :half, edge:], left_in.at[:, :half, :], 0, 1)]
    second.append(bulk(DOWN_2, tiles.at[:, edge:, :half], up_in.at[:, :, :half], 1, 0))

    dy, dx = settings[2, row, col], settings[3, row, col]
    wide = lax.broadcasted_iota(jnp.int32, (BLOCK, LANES), 1)

    def shift_plane(p):
        moved[:, 0:SPILL, :] = jnp.zeros((blocks, SPILL, LANES), F32)

        def sideways(k, carry):
            start = pl.multiple_of(k * BLOCK, BLOCK)
            before = None
            for v in range(blocks):
                x = raw[p, pl.ds(start, BLOCK), v * LANES : (v + 1) * LANES].astype(F32)
                now = pltpu.roll(x, dx, 1)
                out = now if before is None else jnp.where(wide < dx, before, now)
                moved[v, pl.ds(start + SPILL, BLOCK), :] = out
                before = now
            return carry

        lax.fori_loop(0, blocks, sideways, 0)

        def downwards(k, carry):
            start = pl.multiple_of(k * BLOCK, BLOCK)
            for v in range(blocks):
                x = moved[v, pl.ds(start + SPILL - dy, BLOCK), :]
                shifted[p, pl.ds(start, BLOCK), v * LANES : (v + 1) * LANES] = x.astype(shifted.dtype)
            return carry

        lax.fori_loop(0, blocks, downwards, 0)

    for k, (r, c) in enumerate(BLENDED):
        tile_row, tile_col = jnp.maximum(row + r, 0), jnp.maximum(col + c, 0)
        low, high = settings[4, tile_row, tile_col] * BLOCK, settings[5, tile_row, tile_col] * BLOCK
        entries = (
            settings[2, tile_row, tile_col],
            settings[3, tile_row, tile_col],
            jnp.maximum(low, 0),
            jnp.where(exists(r, c), jnp.minimum(high, tile), 0),
        )
        for q, entry in enumerate(entries):
            places[4 * k + q : 4 * k + q + 1, :] = jnp.broadcast_to(entry, (1, LANES))

    for absent, ref in ((col == 0, left_in), (row == 0, up_in), ((row == 0) | (col == 0), corner_in)):

        @pl.when(absent)
        def _(ref=ref):
            ref[...] = jnp.zeros_like(ref)

    shift_plane(0)

    for copy in early:
        copy.wait_recv()

    def covariance(side):
        rows = []
        for p in range(PLANES):
            k = 64 * p + 3 * opposite[side]
            pair = (
                jnp.broadcast_to(means[side][p], (8, LANES)),
                jnp.broadcast_to(stats_in[side][:, k : k + 1], (8, LANES)),
            )
            if side == 0:
                rows.append(cov_tall(raw, 0, edge, half_r, 0, half, pair, p, windows[side]))
            elif side == 1:
                rows.append(cov_tall(raw, half, 0, left_in, half, half, pair, p, windows[side]))
            elif side == 2:
                rows.append(cov_wide(raw, edge, 0, half_d, 0, half, pair, p, windows[side]))
            else:
                rows.append(cov_wide(raw, 0, half, up_in, half, half, pair, p, windows[side]))
        return rows

    cov_rows = [None] * 4
    for side, copy in ((2, first[3]), (3, first[2])):
        copy.wait_recv()
        cov_rows[side] = covariance(side)
    for side, copy in ((0, first[1]), (1, first[0])):
        copy.wait_recv()
        cov_rows[side] = covariance(side)
    sums = jnp.sum(jnp.concatenate([r for rows in cov_rows for r in rows], axis=0), axis=1, keepdims=True)
    index = lax.broadcasted_iota(jnp.int32, (8, LANES), 0)
    chosen = lanes == 64 * (index & 1) + 3 * lax.shift_right_logical(index, 1) + 2
    cov = jnp.sum(jnp.where(chosen, sums, 0.0), axis=0, keepdims=True)
    packed = packed + cov / count_row
    sums_out[...] = packed
    sums_in[CENTRE] = packed
    spread = []
    for k, (r, c) in enumerate(SOURCES):
        copy = Remote(sums_out, sums_in.at[slot_of(r, c)], sums_send.at[k], sums_recv.at[k], -r, -c)
        copy.start()
        spread.append(copy)

    second.append(bulk(CORNER, left_in.at[:, edge:, :], corner_in, 1, 0, col > 0))

    shift_plane(1)

    for copy in spread:
        copy.wait_recv()

    table = sums_in[:, 0, :]
    table = jnp.transpose(jnp.concatenate([table, table], axis=0))

    def quantity(k):
        return jnp.concatenate([table[k : k + 1, :], table[64 + k : 65 + k, :]], axis=0)

    slot = lax.broadcasted_iota(jnp.int32, (PLANES, LANES), 1)
    slot_row = row + lax.shift_right_logical(slot, 3) - 4
    slot_col = col + (slot & 7) - 4
    inside = (slot_row >= 0) & (slot_row < n_row) & (slot_col >= 0) & (slot_col < n_col)
    valid = (inside & (slot_col < n_col - 1), inside & (slot_row < n_row - 1))
    sides = [quantity(3 * side) for side in range(4)]
    spreads = [quantity(3 * side + 1) for side in range(4)]
    covs = (quantity(2) + ahead(quantity(5), 1), quantity(8) + ahead(quantity(11), 8))
    gain_one, level_one = tile_terms(sides, spreads, covs, valid)
    scale = jnp.exp(gain_one)
    gain_two, level_two = tile_terms(
        [scale * m + level_one for m in sides],
        [scale * (scale * v) for v in spreads],
        (scale * (ahead(scale, 1) * covs[0]), scale * (ahead(scale, 8) * covs[1])),
        valid,
    )
    gain = jnp.exp(gain_one + gain_two)
    level = jnp.exp(gain_two) * level_one + level_two
    for k, (r, c) in enumerate(BLENDED):
        s = slot_of(r, c)
        terms[k, 0:2, :] = jnp.broadcast_to(gain[:, s : s + 1], (PLANES, LANES))
        terms[k, 2:4, :] = jnp.broadcast_to(level[:, s : s + 1], (PLANES, LANES))
    for copy in second:
        copy.wait_recv()
    for copy in (*early, *first, *spread, *second):
        copy.wait_send()


def exchange(tiles, settings):
    planes, tile, _ = tiles.shape
    dtype = tiles.dtype
    half = tile // 2
    blocks = tile // LANES
    in_vmem = pl.BlockSpec(memory_space=pltpu.VMEM)
    one = pltpu.VMEM((1, LANES), F32)
    dma = pltpu.SemaphoreType.DMA
    return pl.pallas_call(
        exchange_kernel,
        name="exchange",
        out_shape=(
            jax.ShapeDtypeStruct((planes, tile, tile), dtype),
            jax.ShapeDtypeStruct((planes, tile, STRIP), dtype),
            jax.ShapeDtypeStruct((planes, STRIP, tile), dtype),
            jax.ShapeDtypeStruct((planes, STRIP, STRIP), dtype),
            jax.ShapeDtypeStruct((4, 4, LANES), F32),
            jax.ShapeDtypeStruct((16, LANES), jnp.int32),
        ),
        in_specs=[pl.BlockSpec(memory_space=pl.ANY)] * 2,
        out_specs=(in_vmem,) * 6,
        scratch_shapes=[
            pltpu.SMEM(settings.shape, settings.dtype),
            pltpu.VMEM((planes, tile, tile), dtype),
            pltpu.VMEM((planes, half, STRIP), dtype),
            pltpu.VMEM((planes, STRIP, half), dtype),
            pltpu.VMEM((blocks, SPILL + tile, LANES), F32),
            one,
            pltpu.VMEM((4, 1, LANES), F32),
            one,
            pltpu.VMEM((64, 1, LANES), F32),
            dma((blocks + 1,)),
            dma((7,)),
            dma((7,)),
            dma((4,)),
            dma((4,)),
            dma((len(SOURCES),)),
            dma((len(SOURCES),)),
        ],
        compiler_params=pltpu.CompilerParams(
            collective_id=0, has_side_effects=True, vmem_limit_bytes=48 * 1024 * 1024
        ),
    )(settings, tiles)


def fade(ids, limit, tile):
    steps = jnp.minimum(ids, tile - 1 - ids) + 1
    return jnp.where(limit, steps.astype(F32) * (2.0 / tile), 0.0)


def blend_kernel(
    shifted, raw_left, raw_up, raw_corner, terms, places, blended, weights,
    out, out_weight, moved_left, moved_up, moved_corner, sem,
):
    tile = weights.shape[0]
    rows = ROWS
    count = tile // rows
    blocks = tile // LANES
    lanes = lax.broadcasted_iota(jnp.int32, (rows, LANES), 1)
    lines = lax.broadcasted_iota(jnp.int32, (rows, LANES), 0)
    top_lanes = lax.broadcasted_iota(jnp.int32, (SPILL, LANES), 1)
    zeros = jnp.zeros((SPILL, LANES), F32)

    def entry(k, q):
        return places[4 * k + q : 4 * k + q + 1, :]

    def scalar(k, q):
        return jnp.max(entry(k, q))

    def row_fade(k, first):
        i = lines + (first - entry(k, 0))
        return fade(i, (i >= entry(k, 2)) & (i < entry(k, 3)), tile)

    def col_fade(k, first):
        j = lanes[0:1] + (first - entry(k, 1))
        return fade(j, (j >= 0) & (j < tile), tile)

    def corrected(x, k, p):
        return terms[k, p : p + 1, :] * x + terms[k, 2 + p : 3 + p, :]

    left_rows, left_cols = scalar(1, 0), scalar(1, 1)
    up_rows, up_cols = scalar(2, 0), scalar(2, 1)
    corner_rows, corner_cols = scalar(3, 0), scalar(3, 1)
    moved_left[:, 0:SPILL, :] = jnp.zeros((PLANES, SPILL, LANES), F32)
    columns = [col_fade(0, v * LANES) for v in range(blocks)]
    left_column = col_fade(1, tile)

    def outgoing(first):
        here = pl.ds(first, rows)
        k = first // rows
        return (
            pltpu.make_async_copy(out.at[:, here, :], blended.at[:, here, :], sem.at[0, k]),
            pltpu.make_async_copy(out_weight.at[here, :], weights.at[here, :], sem.at[1, k]),
        )

    def turn_left(first):
        for p in range(PLANES):
            x = pltpu.roll(raw_left[p, pl.ds(first, rows), :].astype(F32), left_cols, 1)
            moved_left[p, pl.ds(first + SPILL, rows), :] = x

    def own_and_left(first):
        here = pl.ds(first, rows)
        own = row_fade(0, first)
        for v in range(blocks):
            weight = own * columns[v]
            part = slice(v * LANES, (v + 1) * LANES)
            values = [
                corrected(shifted[p, here, part].astype(F32), 0, p) * weight for p in range(PLANES)
            ]
            if v == 0:
                other = row_fade(1, first) * left_column
                weight = weight + other
                for p in range(PLANES):
                    x = moved_left[p, pl.ds(first + SPILL - left_rows, rows), :]
                    values[p] = values[p] + corrected(x, 1, p) * other
            out_weight[here, part] = weight
            for p in range(PLANES):
                out[p, here, part] = values[p]

    for k in range(SPILL // rows):
        turn_left(k * rows)

    def below(k, carry):
        first = pl.multiple_of(k * rows, rows)
        turn_left(first)
        own_and_left(first)
        for copy in outgoing(first):
            copy.start()
        return carry

    lax.fori_loop(SPILL // rows, count, below, 0)

    for p in range(PLANES):
        before = None
        for v in range(blocks):
            now = pltpu.roll(raw_up[p, :, v * LANES : (v + 1) * LANES].astype(F32), up_cols, 1)
            moved_up[p, v, 0:SPILL, :] = now if before is None else jnp.where(top_lanes < up_cols, before, now)
            moved_up[p, v, SPILL:, :] = zeros
            before = now
        moved_corner[p, 0:SPILL, :] = pltpu.roll(raw_corner[p].astype(F32), corner_cols, 1)
        moved_corner[p, SPILL:, :] = zeros
    up_columns = [col_fade(2, v * LANES) for v in range(blocks)]
    corner_column = col_fade(3, tile)
    for k in range(SPILL // rows):
        first = k * rows
        here = slice(first, first + rows)
        own_and_left(first)
        upper = row_fade(2, tile + first)
        for v in range(blocks):
            part = slice(v * LANES, (v + 1) * LANES)
            weight = upper * up_columns[v]
            out_weight[here, part] += weight
            for p in range(PLANES):
                x = moved_up[p, v, pl.ds(SPILL + first - up_rows, rows), :]
                out[p, here, part] += corrected(x, 2, p) * weight
        part = slice(0, LANES)
        weight = row_fade(3, tile + first) * corner_column
        out_weight[here, part] += weight
        for p in range(PLANES):
            x = moved_corner[p, pl.ds(SPILL + first - corner_rows, rows), :]
            out[p, here, part] += corrected(x, 3, p) * weight
        for copy in outgoing(first):
            copy.start()
    for k in range(count):
        for copy in outgoing(k * rows):
            copy.wait()


def blend(shifted, left_in, up_in, corner_in, terms, places):
    planes, tile, _ = shifted.shape
    blocks = tile // LANES
    return pl.pallas_call(
        blend_kernel,
        name="blend",
        out_shape=(
            jax.ShapeDtypeStruct((planes, tile, tile), F32),
            jax.ShapeDtypeStruct((tile, tile), F32),
        ),
        in_specs=[pl.BlockSpec(memory_space=pltpu.VMEM)] * 6,
        out_specs=(pl.BlockSpec(memory_space=pl.ANY),) * 2,
        scratch_shapes=[
            pltpu.VMEM((planes, tile, tile), F32),
            pltpu.VMEM((tile, tile), F32),
            pltpu.VMEM((planes, SPILL + tile, LANES), F32),
            pltpu.VMEM((planes, blocks, 2 * SPILL, LANES), F32),
            pltpu.VMEM((planes, 2 * SPILL, LANES), F32),
            pltpu.SemaphoreType.DMA((2, tile // ROWS)),
        ],
        compiler_params=pltpu.CompilerParams(vmem_limit_bytes=32 * 1024 * 1024),
    )(shifted, left_in, up_in, corner_in, terms, places)


def local(tiles, extents, offsets, bands):
    return blend(*exchange(tiles, jnp.concatenate([extents, offsets, bands])))


def solution(mesh):
    return jax.shard_map(
        local,
        mesh=mesh,
        in_specs=(P(None, "row", "col"), P(), P(), P()),
        out_specs=(P(None, "row", "col"), P("row", "col")),
        check_vma=False,
    )
```

```python
import jax
import jax.numpy as jnp
from jax import lax
from jax.experimental import pallas as pl
from jax.experimental.pallas import tpu as pltpu
from jax.sharding import PartitionSpec as P

STRIP = 128
SPILL = 128
BLOCK = 128
LANES = 128
ROWS = 64
PLANES = 2
TILE = 1024
EPS = 1e-6
MESH = pl.DeviceIdType.MESH
F32 = jnp.float32

CENTRE = 36
BLENDED = ((0, 0), (0, -1), (-1, 0), (-1, -1))
SOURCES = tuple(
    (r, c)
    for r in range(-3, 3)
    for c in range(-3, 3)
    if min(abs(r - a) + abs(c - b) for a, b in BLENDED) <= 2 and (r, c) != (0, 0)
)
SOURCES = tuple(sorted(SOURCES, key=lambda d: (-abs(d[0]) - abs(d[1]), d)))
RIGHT_1, LEFT_1, DOWN_1, UP_1, RIGHT_2, DOWN_2, CORNER = range(7)


def slot_of(r, c):
    return CENTRE + 8 * r + c


def total(x):
    return jnp.sum(x, keepdims=True)


def fold(x):
    return jnp.sum(x.reshape(x.shape[0] // 8, 8, x.shape[1]), axis=0)


def sum_tall(ref, plane, first, mask, term):
    size = 128

    def body(i, acc):
        part = pl.ds(pl.multiple_of(i * size, size), size)
        x = ref[plane, part, first : first + STRIP].astype(F32)
        return acc + fold(term(x))

    acc = lax.fori_loop(0, ref.shape[1] // size, body, jnp.zeros((8, LANES), F32))
    return total(jnp.where(mask, acc, 0.0))


def sum_wide(ref, plane, first, extent, term):
    size = 16
    ids = lax.broadcasted_iota(jnp.int32, (size, LANES), 0)

    def body(i, acc):
        x = ref[plane, pl.ds(pl.multiple_of(first + i * size, size), size), :].astype(F32)
        t = term(x)
        part = sum(t[:, k : k + LANES] for k in range(0, x.shape[1], LANES))
        return acc + fold(jnp.where(ids + i * size < extent, part, 0.0))

    return total(lax.fori_loop(0, STRIP // size, body, jnp.zeros((8, LANES), F32)))


def cov_tall(own, row, col, other, other_row, count, means, plane, mask):
    size = 128
    acc = jnp.zeros((8, LANES), F32)
    for start in range(0, count, size):
        x = own[plane, row + start : row + start + size, col : col + STRIP].astype(F32)
        y = other[plane, other_row + start : other_row + start + size, :].astype(F32)
        x = x.reshape(size // 8, 8, LANES) - means[0][None]
        y = y.reshape(size // 8, 8, LANES) - means[1][None]
        acc = acc + jnp.sum(x * y, axis=0)
    return jnp.sum(jnp.where(mask, acc, 0.0), axis=0, keepdims=True)


def cov_wide(own, row, col, other, other_col, count, means, plane, extent):
    size = 16
    ids = lax.broadcasted_iota(jnp.int32, (8, LANES), 0)
    acc = jnp.zeros((8, LANES), F32)
    for start in range(0, STRIP, size):
        part = jnp.zeros((size // 8, 8, LANES), F32)
        for k in range(0, count, LANES):
            x = own[plane, row + start : row + start + size, col + k : col + k + LANES].astype(F32)
            y = other[plane, start : start + size, other_col + k : other_col + k + LANES].astype(F32)
            x = x.reshape(size // 8, 8, LANES) - means[0][None]
            y = y.reshape(size // 8, 8, LANES) - means[1][None]
            part = part + x * y
        for k in range(size // 8):
            acc = acc + jnp.where(ids + (start + 8 * k) < extent, part[k], 0.0)
    return jnp.sum(acc, axis=0, keepdims=True)


def pair_terms(mean_a, var_a, mean_b, var_b, cov, valid):
    weight = cov * cov / ((var_a + EPS) * (var_b + EPS))
    ratio = 0.25 * (jnp.log(var_b + EPS) - jnp.log(var_a + EPS))
    shift = 0.5 * (mean_b - mean_a)
    return tuple(jnp.where(valid, t, 0.0) for t in (weight, weight * ratio, weight * shift))


def ahead(x, distance):
    return pltpu.roll(x, (LANES - distance) % LANES, 1)


def tile_terms(means, variances, covs, valid):
    across = pair_terms(means[0], variances[0], ahead(means[1], 1), ahead(variances[1], 1), covs[0], valid[0])
    along = pair_terms(means[2], variances[2], ahead(means[3], 8), ahead(variances[3], 8), covs[1], valid[1])
    back = [ahead(t, -1) for t in across]
    above = [ahead(t, -8) for t in along]
    scale = 1.0 + across[0] + along[0] + back[0] + above[0]
    return tuple((across[k] + along[k] - back[k] - above[k]) / scale for k in (1, 2))


def fade(ids, limit, tile):
    steps = jnp.minimum(ids, tile - 1 - ids) + 1
    return jnp.where(limit, steps.astype(F32) * (2.0 / tile), 0.0)


def row_fade(places, k, lines):
    i = lines - places[4 * k : 4 * k + 1, :]
    return fade(i, (i >= places[4 * k + 2 : 4 * k + 3, :]) & (i < places[4 * k + 3 : 4 * k + 4, :]), TILE)


def col_fade(places, k, columns):
    j = columns - places[4 * k + 1 : 4 * k + 2, :]
    return fade(j, (j >= 0) & (j < TILE), TILE)


def exchange_kernel(
    settings_in, tiles, shifted, total_weight, left_in, up_in, corner_in, terms, places,
    settings, raw, half_r, half_d, moved, stats_out, stats_in, sums_out, sums_in,
    load_sem, send_sem, recv_sem, mean_send, mean_recv, sums_send, sums_recv, rounds,
):
    n_col, n_row = lax.axis_size("col"), lax.axis_size("row")
    col, row = lax.axis_index("col"), lax.axis_index("row")
    tile = raw.shape[1]
    half = tile // 2
    edge = tile - STRIP
    blocks = tile // LANES
    four = ((0, 1), (0, -1), (1, 0), (-1, 0))

    def exists(r, c):
        return (row + r >= 0) & (row + r < n_row) & (col + c >= 0) & (col + c < n_col)

    def place(r, c):
        return {"row": row + r, "col": col + c}

    sums_in[...] = jnp.zeros_like(sums_in)
    stats_in[...] = jnp.zeros_like(stats_in)

    def tell(semaphore):
        for r, c in four:

            @pl.when(exists(r, c))
            def _(r=r, c=c):
                pl.semaphore_signal(semaphore, inc=1, device_id=place(r, c), device_id_type=MESH)

    neighbours = sum(exists(r, c).astype(jnp.int32) for r, c in four)
    barrier = pltpu.get_barrier_semaphore()
    tell(barrier)

    fetch = pltpu.make_async_copy(settings_in, settings, load_sem.at[blocks])
    fetch.start()
    loads = []
    for k in range(blocks):
        part = pl.ds(k * BLOCK, BLOCK)
        loads.append(pltpu.make_async_copy(tiles.at[:, part, :], raw.at[:, part, :], load_sem.at[k]))
        loads[k].start()

    pl.semaphore_wait(barrier, neighbours)

    class Remote:
        def __init__(self, src, dst, send, recv, r, c, wanted=True):
            self.there, self.here = exists(r, c) & wanted, exists(-r, -c) & wanted
            self.copy = pltpu.make_async_remote_copy(
                src_ref=src,
                dst_ref=dst,
                send_sem=send,
                recv_sem=recv,
                device_id=place(r, c),
                device_id_type=MESH,
            )

        def start(self):
            pl.when(self.there)(self.copy.start)

        def wait_recv(self):
            pl.when(self.here)(self.copy.wait_recv)

        def wait_send(self):
            pl.when(self.there)(self.copy.wait_send)

    def bulk(index, src, dst, r, c, wanted=True):
        copy = Remote(src, dst, send_sem.at[index], recv_sem.at[index], r, c, wanted)
        copy.start()
        return copy

    first = [
        bulk(RIGHT_1, tiles.at[:, half:, edge:], left_in.at[:, half:, :], 0, 1),
        bulk(LEFT_1, tiles.at[:, :half, :STRIP], half_r, 0, -1),
        bulk(DOWN_1, tiles.at[:, edge:, half:], up_in.at[:, :, half:], 1, 0),
        bulk(UP_1, tiles.at[:, :STRIP, :half], half_d, -1, 0),
    ]

    fetch.wait()
    ext = (
        settings[0, row, col],
        settings[0, row, jnp.maximum(col - 1, 0)],
        settings[1, row, col],
        settings[1, jnp.maximum(row - 1, 0), col],
    )
    lanes = lax.broadcasted_iota(jnp.int32, (8, LANES), 1)
    windows = (lanes < ext[0], lanes < ext[1], ext[2], ext[3])
    numbers = [(e * tile).astype(F32) for e in ext]
    one = lax.broadcasted_iota(jnp.int32, (1, LANES), 1)

    tell(rounds.at[0])
    for load in loads:
        load.wait()

    means = []
    packed = jnp.zeros((1, LANES), F32)
    count_row = jnp.ones((1, LANES), F32)
    for side in range(4):
        reduce = sum_tall if side < 2 else sum_wide
        begin = edge if side in (0, 2) else 0
        own_means = []
        for p in range(PLANES):
            mean = reduce(raw, p, begin, windows[side], lambda x: x) / numbers[side]

            def square(x, mean=mean):
                return (x - mean) * (x - mean)

            var = reduce(raw, p, begin, windows[side], square) / numbers[side]
            packed = jnp.where(one == 64 * p + 3 * side, mean, packed)
            packed = jnp.where(one == 64 * p + 3 * side + 1, var, packed)
            count_row = jnp.where(one == 64 * p + 3 * side + 2, numbers[side], count_row)
            own_means.append(mean)
        means.append(own_means)
        if side in (1, 3):
            pl.semaphore_wait(rounds.at[side // 2], neighbours)
            tell(rounds.at[side // 2 + 1])
    stats_out[...] = packed
    opposite = (1, 0, 3, 2)
    early = []
    for side, (r, c) in enumerate(four):
        early.append(
            Remote(stats_out, stats_in.at[opposite[side]], mean_send.at[side], mean_recv.at[opposite[side]], r, c)
        )
        early[side].start()

    second = [bulk(RIGHT_2, tiles.at[:, :half, edge:], left_in.at[:, :half, :], 0, 1)]
    second.append(bulk(DOWN_2, tiles.at[:, edge:, :half], up_in.at[:, :, :half], 1, 0))

    dy, dx = settings[2, row, col], settings[3, row, col]
    wide = lax.broadcasted_iota(jnp.int32, (BLOCK, LANES), 1)

    def weigh():
        size = 64
        lines = lax.broadcasted_iota(jnp.int32, (size, LANES), 0)
        columns = lax.broadcasted_iota(jnp.int32, (1, LANES), 1)
        own = [col_fade(places, 0, columns + v * LANES) for v in range(blocks)]
        side = col_fade(places, 1, columns + tile)

        def body(k, carry):
            here = pl.ds(pl.multiple_of(k * size, size), size)
            fades = row_fade(places, 0, lines + k * size)
            beside = row_fade(places, 1, lines + k * size)
            for v in range(blocks):
                weight = fades * own[v]
                if v == 0:
                    weight = weight + beside * side
                total_weight[here, v * LANES : (v + 1) * LANES] = weight
            return carry

        lax.fori_loop(0, tile // size, body, 0)
        above = [col_fade(places, 2, columns + v * LANES) for v in range(blocks)]
        corner = col_fade(places, 3, columns + tile)
        for first in range(0, SPILL, size):
            fades = row_fade(places, 2, lines + (tile + first))
            beside = row_fade(places, 3, lines + (tile + first))
            for v in range(blocks):
                weight = fades * above[v]
                if v == 0:
                    weight = weight + beside * corner
                total_weight[first : first + size, v * LANES : (v + 1) * LANES] += weight

    def shift_plane(p):
        moved[:, 0:SPILL, :] = jnp.zeros((blocks, SPILL, LANES), F32)

        def sideways(k, carry):
            start = pl.multiple_of(k * BLOCK, BLOCK)
            before = None
            for v in range(blocks):
                x = raw[p, pl.ds(start, BLOCK), v * LANES : (v + 1) * LANES].astype(F32)
                now = pltpu.roll(x, dx, 1)
                out = now if before is None else jnp.where(wide < dx, before, now)
                moved[v, pl.ds(start + SPILL, BLOCK), :] = out
                before = now
            return carry

        lax.fori_loop(0, blocks, sideways, 0)

        def downwards(k, carry):
            start = pl.multiple_of(k * BLOCK, BLOCK)
            for v in range(blocks):
                x = moved[v, pl.ds(start + SPILL - dy, BLOCK), :]
                shifted[p, pl.ds(start, BLOCK), v * LANES : (v + 1) * LANES] = x.astype(shifted.dtype)
            return carry

        lax.fori_loop(0, blocks, downwards, 0)

    for k, (r, c) in enumerate(BLENDED):
        tile_row, tile_col = jnp.maximum(row + r, 0), jnp.maximum(col + c, 0)
        low, high = settings[4, tile_row, tile_col] * BLOCK, settings[5, tile_row, tile_col] * BLOCK
        entries = (
            settings[2, tile_row, tile_col],
            settings[3, tile_row, tile_col],
            jnp.maximum(low, 0),
            jnp.where(exists(r, c), jnp.minimum(high, tile), 0),
        )
        for q, entry in enumerate(entries):
            places[4 * k + q : 4 * k + q + 1, :] = jnp.broadcast_to(entry, (1, LANES))

    for absent, ref in ((col == 0, left_in), (row == 0, up_in), ((row == 0) | (col == 0), corner_in)):

        @pl.when(absent)
        def _(ref=ref):
            ref[...] = jnp.zeros_like(ref)

    shift_plane(0)
    weigh()

    pl.semaphore_wait(rounds.at[2], neighbours)
    for copy in early:
        copy.wait_recv()

    def covariance(side):
        rows = []
        for p in range(PLANES):
            k = 64 * p + 3 * opposite[side]
            pair = (
                jnp.broadcast_to(means[side][p], (8, LANES)),
                jnp.broadcast_to(stats_in[side][:, k : k + 1], (8, LANES)),
            )
            if side == 0:
                rows.append(cov_tall(raw, 0, edge, half_r, 0, half, pair, p, windows[side]))
            elif side == 1:
                rows.append(cov_tall(raw, half, 0, left_in, half, half, pair, p, windows[side]))
            elif side == 2:
                rows.append(cov_wide(raw, edge, 0, half_d, 0, half, pair, p, windows[side]))
            else:
                rows.append(cov_wide(raw, 0, half, up_in, half, half, pair, p, windows[side]))
        return rows

    cov_rows = [None] * 4
    for side, copy in ((2, first[3]), (3, first[2])):
        copy.wait_recv()
        cov_rows[side] = covariance(side)
    for side, copy in ((0, first[1]), (1, first[0])):
        copy.wait_recv()
        cov_rows[side] = covariance(side)
    sums = jnp.sum(jnp.concatenate([r for rows in cov_rows for r in rows], axis=0), axis=1, keepdims=True)
    index = lax.broadcasted_iota(jnp.int32, (8, LANES), 0)
    chosen = lanes == 64 * (index & 1) + 3 * lax.shift_right_logical(index, 1) + 2
    cov = jnp.sum(jnp.where(chosen, sums, 0.0), axis=0, keepdims=True)
    packed = packed + cov / count_row
    sums_out[...] = packed
    sums_in[CENTRE] = packed
    spread = []
    for k, (r, c) in enumerate(SOURCES):
        copy = Remote(sums_out, sums_in.at[slot_of(r, c)], sums_send.at[k], sums_recv.at[k], -r, -c)
        copy.start()
        spread.append(copy)

    second.append(bulk(CORNER, left_in.at[:, edge:, :], corner_in, 1, 0, col > 0))

    shift_plane(1)

    for copy in spread:
        copy.wait_recv()

    table = sums_in[:, 0, :]
    table = jnp.transpose(jnp.concatenate([table, table], axis=0))

    def quantity(k):
        return jnp.concatenate([table[k : k + 1, :], table[64 + k : 65 + k, :]], axis=0)

    slot = lax.broadcasted_iota(jnp.int32, (PLANES, LANES), 1)
    slot_row = row + lax.shift_right_logical(slot, 3) - 4
    slot_col = col + (slot & 7) - 4
    inside = (slot_row >= 0) & (slot_row < n_row) & (slot_col >= 0) & (slot_col < n_col)
    valid = (inside & (slot_col < n_col - 1), inside & (slot_row < n_row - 1))
    sides = [quantity(3 * side) for side in range(4)]
    spreads = [quantity(3 * side + 1) for side in range(4)]
    covs = (quantity(2) + ahead(quantity(5), 1), quantity(8) + ahead(quantity(11), 8))
    gain_one, level_one = tile_terms(sides, spreads, covs, valid)
    scale = jnp.exp(gain_one)
    gain_two, level_two = tile_terms(
        [scale * m + level_one for m in sides],
        [scale * (scale * v) for v in spreads],
        (scale * (ahead(scale, 1) * covs[0]), scale * (ahead(scale, 8) * covs[1])),
        valid,
    )
    gain = jnp.exp(gain_one + gain_two)
    level = jnp.exp(gain_two) * level_one + level_two
    for k, (r, c) in enumerate(BLENDED):
        s = slot_of(r, c)
        terms[k, 0:2, :] = jnp.broadcast_to(gain[:, s : s + 1], (PLANES, LANES))
        terms[k, 2:4, :] = jnp.broadcast_to(level[:, s : s + 1], (PLANES, LANES))
    for copy in second:
        copy.wait_recv()
    for copy in (*early, *first, *spread, *second):
        copy.wait_send()


def exchange(tiles, settings):
    planes, tile, _ = tiles.shape
    dtype = tiles.dtype
    half = tile // 2
    blocks = tile // LANES
    in_vmem = pl.BlockSpec(memory_space=pltpu.VMEM)
    one = pltpu.VMEM((1, LANES), F32)
    dma = pltpu.SemaphoreType.DMA
    return pl.pallas_call(
        exchange_kernel,
        name="exchange",
        out_shape=(
            jax.ShapeDtypeStruct((planes, tile, tile), dtype),
            jax.ShapeDtypeStruct((tile, tile), F32),
            jax.ShapeDtypeStruct((planes, tile, STRIP), dtype),
            jax.ShapeDtypeStruct((planes, STRIP, tile), dtype),
            jax.ShapeDtypeStruct((planes, STRIP, STRIP), dtype),
            jax.ShapeDtypeStruct((4, 4, LANES), F32),
            jax.ShapeDtypeStruct((16, LANES), jnp.int32),
        ),
        in_specs=[pl.BlockSpec(memory_space=pl.ANY)] * 2,
        out_specs=(in_vmem,) * 7,
        scratch_shapes=[
            pltpu.SMEM(settings.shape, settings.dtype),
            pltpu.VMEM((planes, tile, tile), dtype),
            pltpu.VMEM((planes, half, STRIP), dtype),
            pltpu.VMEM((planes, STRIP, half), dtype),
            pltpu.VMEM((blocks, SPILL + tile, LANES), F32),
            one,
            pltpu.VMEM((4, 1, LANES), F32),
            one,
            pltpu.VMEM((64, 1, LANES), F32),
            dma((blocks + 1,)),
            dma((7,)),
            dma((7,)),
            dma((4,)),
            dma((4,)),
            dma((len(SOURCES),)),
            dma((len(SOURCES),)),
            pltpu.SemaphoreType.REGULAR((3,)),
        ],
        compiler_params=pltpu.CompilerParams(
            collective_id=0, has_side_effects=True, vmem_limit_bytes=44 * 1024 * 1024
        ),
    )(settings, tiles)


def blend_kernel(
    shifted, total_weight, raw_left, raw_up, raw_corner, terms, places, blended, weights,
    out, moved_left, moved_up, moved_corner, sem,
):
    whole = pltpu.make_async_copy(total_weight, weights, sem.at[weights.shape[0] // ROWS])
    whole.start()
    tile = weights.shape[0]
    rows = ROWS
    count = tile // rows
    blocks = tile // LANES
    lanes = lax.broadcasted_iota(jnp.int32, (rows, LANES), 1)
    lines = lax.broadcasted_iota(jnp.int32, (rows, LANES), 0)
    top_lanes = lax.broadcasted_iota(jnp.int32, (SPILL, LANES), 1)
    zeros = jnp.zeros((SPILL, LANES), F32)

    def scalar(k, q):
        return jnp.max(places[4 * k + q : 4 * k + q + 1, :])

    def corrected(x, k, p):
        return terms[k, p : p + 1, :] * x + terms[k, 2 + p : 3 + p, :]

    left_rows, left_cols = scalar(1, 0), scalar(1, 1)
    up_rows, up_cols = scalar(2, 0), scalar(2, 1)
    corner_rows, corner_cols = scalar(3, 0), scalar(3, 1)
    moved_left[:, 0:SPILL, :] = jnp.zeros((PLANES, SPILL, LANES), F32)
    columns = [col_fade(places, 0, lanes[0:1] + v * LANES) for v in range(blocks)]
    left_column = col_fade(places, 1, lanes[0:1] + tile)

    def outgoing(first):
        here = pl.ds(first, rows)
        return pltpu.make_async_copy(out.at[:, here, :], blended.at[:, here, :], sem.at[first // rows])

    def turn_left(first):
        for p in range(PLANES):
            x = pltpu.roll(raw_left[p, pl.ds(first, rows), :].astype(F32), left_cols, 1)
            moved_left[p, pl.ds(first + SPILL, rows), :] = x

    def own_and_left(first):
        here = pl.ds(first, rows)
        own = row_fade(places, 0, lines + first)
        for v in range(blocks):
            weight = own * columns[v]
            part = slice(v * LANES, (v + 1) * LANES)
            values = [
                corrected(shifted[p, here, part].astype(F32), 0, p) * weight for p in range(PLANES)
            ]
            if v == 0:
                other = row_fade(places, 1, lines + first) * left_column
                for p in range(PLANES):
                    x = moved_left[p, pl.ds(first + SPILL - left_rows, rows), :]
                    values[p] = values[p] + corrected(x, 1, p) * other
            for p in range(PLANES):
                out[p, here, part] = values[p]

    for k in range(SPILL // rows):
        turn_left(k * rows)

    def below(k, carry):
        first = pl.multiple_of(k * rows, rows)
        turn_left(first)
        own_and_left(first)
        outgoing(first).start()
        return carry

    lax.fori_loop(SPILL // rows, count, below, 0)

    for p in range(PLANES):
        before = None
        for v in range(blocks):
            now = pltpu.roll(raw_up[p, :, v * LANES : (v + 1) * LANES].astype(F32), up_cols, 1)
            moved_up[p, v, 0:SPILL, :] = now if before is None else jnp.where(top_lanes < up_cols, before, now)
            moved_up[p, v, SPILL:, :] = zeros
            before = now
        moved_corner[p, 0:SPILL, :] = pltpu.roll(raw_corner[p].astype(F32), corner_cols, 1)
        moved_corner[p, SPILL:, :] = zeros
    up_columns = [col_fade(places, 2, lanes[0:1] + v * LANES) for v in range(blocks)]
    corner_column = col_fade(places, 3, lanes[0:1] + tile)
    for k in range(SPILL // rows):
        first = k * rows
        here = slice(first, first + rows)
        own_and_left(first)
        upper = row_fade(places, 2, lines + (tile + first))
        for v in range(blocks):
            part = slice(v * LANES, (v + 1) * LANES)
            weight = upper * up_columns[v]
            for p in range(PLANES):
                x = moved_up[p, v, pl.ds(SPILL + first - up_rows, rows), :]
                out[p, here, part] += corrected(x, 2, p) * weight
        part = slice(0, LANES)
        weight = row_fade(places, 3, lines + (tile + first)) * corner_column
        for p in range(PLANES):
            x = moved_corner[p, pl.ds(SPILL + first - corner_rows, rows), :]
            out[p, here, part] += corrected(x, 3, p) * weight
        outgoing(first).start()
    for k in range(count):
        outgoing(k * rows).wait()
    whole.wait()


def blend(shifted, total_weight, left_in, up_in, corner_in, terms, places):
    planes, tile, _ = shifted.shape
    blocks = tile // LANES
    return pl.pallas_call(
        blend_kernel,
        name="blend",
        out_shape=(
            jax.ShapeDtypeStruct((planes, tile, tile), F32),
            jax.ShapeDtypeStruct((tile, tile), F32),
        ),
        in_specs=[pl.BlockSpec(memory_space=pltpu.VMEM)] * 7,
        out_specs=(pl.BlockSpec(memory_space=pl.ANY),) * 2,
        scratch_shapes=[
            pltpu.VMEM((planes, tile, tile), F32),
            pltpu.VMEM((planes, SPILL + tile, LANES), F32),
            pltpu.VMEM((planes, blocks, 2 * SPILL, LANES), F32),
            pltpu.VMEM((planes, 2 * SPILL, LANES), F32),
            pltpu.SemaphoreType.DMA((tile // ROWS + 1,)),
        ],
        compiler_params=pltpu.CompilerParams(vmem_limit_bytes=32 * 1024 * 1024),
    )(shifted, total_weight, left_in, up_in, corner_in, terms, places)


def local(tiles, extents, offsets, bands):
    return blend(*exchange(tiles, jnp.concatenate([extents, offsets, bands])))


def solution(mesh):
    return jax.shard_map(
        local,
        mesh=mesh,
        in_specs=(P(None, "row", "col"), P(), P(), P()),
        out_specs=(P(None, "row", "col"), P("row", "col")),
        check_vma=False,
    )
```
